512 devices in a mesh: group: 32 (over y_lo, z), tensor: 16 (over y_hi, x, core).
Axes of the slice: x: 4, y: 4 (y_hi: 2, y_lo: 2; y = y_hi * 2 + y_lo), z: 16, core: 2. Of those that a mesh axis runs over, the one named last changes fastest.
Arguments:
- queries: bfloat16 [4, 256, 4096], P(None, 'group', 'tensor')
- key_cache_rows: bfloat16 [256, 16, 512, 128], P('group', 'tensor'), as said below
- value_cache_rows: bfloat16 [256, 16, 512, 128], P('group', 'tensor'), as said below
- step_keys: bfloat16 [4, 256, 16, 128], P(None, 'group', 'tensor'), as said below
- step_values: bfloat16 [4, 256, 16, 128], P(None, 'group', 'tensor'), as said below
- lengths: int32 [256], P('group'), may hold values from 2 to 512, as said below
- output_weight: bfloat16 [4096, 5120], P('tensor'), may hold values from -0.125 to 0.125
- adapter_down_weight: bfloat16 [4096, 64], P('tensor', 'group'), may hold values from -0.09375 to 0.09375
- adapter_up_weight: bfloat16 [64, 5120], P('group', 'tensor'), may hold values from -0.75 to 0.75
Outputs:
- projected: bfloat16 [4, 256, 5120], P(None, 'group', 'tensor')
The draws below stay inside these ranges and needn't reach their ends.
Inputs may be any that keep to these rules, and one draw needn't show every extreme that they name: `lengths`: each sequence has from 2 to 512 cached positions; some sequence has exactly 512 and some exactly 2. `key_cache_rows`: copies g and g' are equal when g // 4 == g' // 4. `value_cache_rows`: copies g and g' are equal when g // 4 == g' // 4. `step_keys`: copies g and g' are equal when g // 4 == g' // 4. `step_values`: copies g and g' are equal when g // 4 == g' // 4.
All inputs are finite; a program needn't handle non-finite values.
Results may differ from the reference program's by a relative error of at most 0.0057.
Values may be sent and summed in bfloat16 or wider, within the bound.
A program may use at most 64 MiB of HBM per device.

```python
import jax
import jax.numpy as jnp
from jax import lax

MODEL_WIDTH = 5120
HEAD_SIZE = 128
QH = 2
ADAPTER_RANK = 64
STEPS = 4
CACHE = 512
QUERY_HEADS = 32
KV_HEADS = 4
SLOTS = 16
ROWS = 256


def spread_copies(drawn, reduce_axis):
    return jnp.repeat(drawn, SLOTS // KV_HEADS, axis=reduce_axis)


def shared_keys(key):
    drawn = jnp.clip(2.0 * jax.random.normal(key, (ROWS, KV_HEADS, CACHE, HEAD_SIZE), jnp.float32), -9.0, 9.0)
    return spread_copies(drawn, 1)


def draw_key_cache_rows(key, part):
    drawn = shared_keys(key)
    return drawn.astype(jnp.bfloat16)


def draw_queries(key, part):
    key = jax.random.fold_in(key, 2)
    drawn = jax.random.normal(key, (STEPS, ROWS, QUERY_HEADS, HEAD_SIZE), jnp.float32)
    return drawn.reshape(STEPS, ROWS, QUERY_HEADS * HEAD_SIZE).astype(jnp.bfloat16)


def draw_lengths(key, part):
    key = jax.random.fold_in(key, 3)
    first_key, second_key = jax.random.split(key)
    drawn = jax.random.randint(first_key, (ROWS,), 2, CACHE + 1)
    order = jax.random.permutation(second_key, ROWS)
    drawn = jnp.where(jnp.arange(ROWS) == order[0], CACHE, drawn)
    drawn = jnp.where(jnp.arange(ROWS) == order[1], 2, drawn)
    return drawn.astype(jnp.int32)


def draw_value_cache_rows(key, part):
    key = jax.random.fold_in(key, 4)
    drawn = jnp.clip(jax.random.normal(key, (ROWS, KV_HEADS, CACHE, HEAD_SIZE), jnp.float32), -6.0, 6.0)
    return spread_copies(drawn, 1).astype(jnp.bfloat16)


def draw_step_keys(key, part):
    key = jax.random.fold_in(key, 5)
    drawn = jnp.clip(2.0 * jax.random.normal(key, (STEPS, ROWS, KV_HEADS, HEAD_SIZE), jnp.float32), -9.0, 9.0)
    return spread_copies(drawn, 2).astype(jnp.bfloat16)


def draw_step_values(key, part):
    key = jax.random.fold_in(key, 6)
    drawn = jnp.clip(jax.random.normal(key, (STEPS, ROWS, KV_HEADS, HEAD_SIZE), jnp.float32), -6.0, 6.0)
    return spread_copies(drawn, 2).astype(jnp.bfloat16)


def with_spikes(array, stream_key, source, target, shards_of, factor):
    owner, partner = [(jnp.arange(array.shape[dim]) // (array.shape[dim] // shards_of)).reshape([-1 if axis == dim else 1 for axis in range(array.ndim)]) for dim in (source, target)]
    chosen = jax.random.permutation(stream_key, shards_of)[partner]
    strong = (owner == chosen) | (owner == (partner + shards_of // 2) % shards_of)
    return jnp.where(strong, factor * array, array)


def levels(key, shape, cuts, low, top_value):
    def one(position, parts):
        steps = jax.random.uniform(jax.random.fold_in(jax.random.fold_in(key, 6), position), (parts,), jnp.float32, low / len(cuts), top_value / len(cuts))
        return jnp.repeat(jnp.exp(steps), shape[position] // parts).reshape((-1,) + (1,) * (len(shape) - position - 1))

    loudness = one(*cuts[0])
    for cut in cuts[1:]:
        loudness = loudness * one(*cut)
    return loudness


def noise(stream_key, shape, deviation, bound, pieces=(), kind=jnp.bfloat16):
    values = jax.random.normal(stream_key, shape, jnp.float32) * deviation
    if len(pieces) > 0:
        values = levels(stream_key, shape, pieces, -0.22, 0.18) * values
    return jnp.clip(values, min=-bound, max=bound).astype(kind)


def noise_with(key, extent, width, reach, cuts, heavy, dtype=jnp.bfloat16):
    result = width * jax.random.normal(key, extent, jnp.float32)
    if cuts:
        result = result * levels(key, extent, cuts, -0.22, 0.18)
    return jnp.clip(with_spikes(result, jax.random.fold_in(key, 3), *heavy), -reach, reach).astype(dtype)


def setup_inputs(seed: int = 0) -> dict:
    keys = jax.random.split(jax.random.key(seed), 10)
    queries = draw_queries(jax.random.fold_in(keys[9], 71), 0)
    key_cache_rows = draw_key_cache_rows(jax.random.fold_in(keys[9], 71), 0)
    value_cache_rows = draw_value_cache_rows(jax.random.fold_in(keys[9], 71), 0)
    step_keys = draw_step_keys(jax.random.fold_in(keys[9], 71), 0)
    step_values = draw_step_values(jax.random.fold_in(keys[9], 71), 0)
    lengths = draw_lengths(jax.random.fold_in(keys[9], 71), 0)
    output_weight = noise_with(keys[6], (QUERY_HEADS * HEAD_SIZE, MODEL_WIDTH), (QUERY_HEADS * HEAD_SIZE) ** -0.5, 0.125, ((0, 16),), (0, 1, 16, 2.0))
    adapter_down_weight = noise(keys[7], (QUERY_HEADS * HEAD_SIZE, ADAPTER_RANK), (QUERY_HEADS * HEAD_SIZE) ** -0.5, 0.09375, ((0, 16), (1, 32)))
    adapter_up_weight = noise(keys[8], (ADAPTER_RANK, MODEL_WIDTH), ADAPTER_RANK ** -0.5, 0.75, ((0, 32), (1, 16)))
    return {"queries": queries, "key_cache_rows": key_cache_rows, "value_cache_rows": value_cache_rows, "step_keys": step_keys, "step_values": step_values, "lengths": lengths, "output_weight": output_weight, "adapter_down_weight": adapter_down_weight, "adapter_up_weight": adapter_up_weight}


def attend_row(packed):
    query_row, key_rows, value_rows, fresh_keys, fresh_values, length = packed
    step_count = query_row.shape[0]
    score_scale = HEAD_SIZE ** -0.5
    grouped = query_row.reshape(step_count, SLOTS, QH, HEAD_SIZE).astype(jnp.float32)
    cached = jnp.einsum("sgqd,gld->sgql", grouped, key_rows.astype(jnp.float32)) * score_scale
    in_cache = jnp.arange(CACHE)[None, None, None, :] < length
    cached = jnp.where(in_cache, cached, jnp.float32(-1e30))
    recent = jnp.einsum("sgqd,tgd->sgqt", grouped, fresh_keys.astype(jnp.float32)) * score_scale
    causal = jnp.arange(step_count)[None, :] <= jnp.arange(step_count)[:, None]
    recent = jnp.where(causal[:, None, None, :], recent, jnp.float32(-1e30))
    row_top = jnp.maximum(jnp.max(cached, axis=-1, keepdims=True), jnp.max(recent, axis=-1, keepdims=True))
    cached_exp = jnp.exp(cached - row_top)
    recent_exp = jnp.exp(recent - row_top)
    weight_sum = jnp.sum(cached_exp, axis=-1, keepdims=True) + jnp.sum(recent_exp, axis=-1, keepdims=True)
    cached_w = (cached_exp / weight_sum).astype(jnp.bfloat16).astype(jnp.float32)
    recent_w = (recent_exp / weight_sum).astype(jnp.bfloat16).astype(jnp.float32)
    mixed = jnp.einsum("sgql,gld->sgqd", cached_w, value_rows.astype(jnp.float32))
    mixed = mixed + jnp.einsum("sgqt,tgd->sgqd", recent_w, fresh_values.astype(jnp.float32))
    return mixed.astype(jnp.bfloat16).reshape(step_count, SLOTS * QH * HEAD_SIZE)


def reference(queries, key_cache_rows, value_cache_rows, step_keys, step_values, lengths, output_weight, adapter_down_weight, adapter_up_weight):
    step_count = queries.shape[0]
    row_count = queries.shape[1]
    per_row = lax.map(attend_row, (jnp.swapaxes(queries, 0, 1), key_cache_rows, value_cache_rows,
                                   jnp.swapaxes(step_keys, 0, 1), jnp.swapaxes(step_values, 0, 1), lengths))
    attention_output = jnp.swapaxes(per_row, 0, 1).reshape(step_count * row_count, SLOTS * QH * HEAD_SIZE)
    base_terms = jnp.dot(attention_output, output_weight, preferred_element_type=jnp.float32)
    low_rank_output = jnp.dot(attention_output, adapter_down_weight, preferred_element_type=jnp.float32)
    adapter_delta = jnp.dot(low_rank_output, adapter_up_weight.astype(jnp.float32), precision=lax.Precision.HIGHEST)
    projected = (base_terms + 2.0 * adapter_delta).astype(jnp.bfloat16)
    return projected.reshape(step_count, row_count, MODEL_WIDTH)
```

```python
import functools
import math

import jax
import jax.numpy as jnp
from jax import lax
from jax.experimental import pallas as pl
from jax.experimental.pallas import tpu as pltpu
from jax.sharding import PartitionSpec as P

MESH = pl.DeviceIdType.MESH
HEAD_SIZE = 128
QH = 2
EXP2_SCALE = HEAD_SIZE**-0.5 / math.log(2.0)
NEG = -1e30
VMEM_BYTES = 63 * 1024 * 1024


def nt_dot(a, b):
    return lax.dot_general(a, b, (((1,), (1,)), ((), ())), preferred_element_type=jnp.float32)


def kernel(
    groups,
    tensors,
    q_hbm,
    k_hbm,
    v_hbm,
    sk_hbm,
    sv_hbm,
    len_hbm,
    w_hbm,
    down_hbm,
    up_hbm,
    out_ref,
    q_v,
    k_v,
    v_v,
    sk_v,
    sv_v,
    len_v,
    w_v,
    down_v,
    up_v,
    gath,
    factors,
    keep,
    send1,
    recv1,
    send2,
    recv2,
    small_sem,
    k_sem,
    v_sem,
    w_sem,
    gsend_sem,
    grecv_sem,
    s1_sem,
    r1_sem,
    s2_sem,
    r2_sem,
):
    steps, rows, _ = q_v.shape
    cache = k_v.shape[0]
    toks = steps * rows
    cols = out_ref.shape[2]
    depth = down_v.shape[1]
    chips = tensors // 2
    rank = factors.shape[0]

    g = lax.axis_index("group")
    t = lax.axis_index("tensor")
    chip = t // 2
    core = t % 2

    smalls = [
        pltpu.make_async_copy(src, dst, small_sem.at[i])
        for i, (src, dst) in enumerate(
            [
                (down_hbm, down_v),
                (up_hbm, up_v),
                (q_hbm, q_v),
                (sk_hbm, sk_v),
                (sv_hbm, sv_v),
                (len_hbm, len_v),
            ]
        )
    ]
    for c in smalls:
        c.start()
    k_copies = [
        pltpu.make_async_copy(k_hbm.at[r], k_v.at[:, pl.ds(r * HEAD_SIZE, HEAD_SIZE)], k_sem.at[r])
        for r in range(rows)
    ]
    v_copies = [
        pltpu.make_async_copy(v_hbm.at[r], v_v.at[pl.ds(r * cache, cache)], v_sem.at[r])
        for r in range(rows)
    ]
    pair = 2 * cols

    def chunk_at(k):
        return lax.rem(chip + k + 1, chips)

    w_copies = [
        pltpu.make_async_copy(
            w_hbm.at[:, pl.ds(pl.multiple_of(chunk_at(k) * pair, 128), pair)], w_v.at[k], w_sem.at[k]
        )
        for k in range(chips)
    ]
    for c in k_copies + v_copies + w_copies:
        c.start()

    barrier = pltpu.get_barrier_semaphore()

    def greet_group(d, carry):
        pl.semaphore_signal(
            barrier, inc=1, device_id={"group": lax.rem(g + d, groups)}, device_id_type=MESH
        )
        return carry

    lax.fori_loop(1, groups, greet_group, 0)
    pl.semaphore_signal(barrier, inc=1, device_id={"tensor": t + 1 - 2 * core}, device_id_type=MESH)
    for k in range(chips - 1):
        pl.semaphore_signal(
            barrier, inc=1, device_id={"tensor": chunk_at(k) * 2 + core}, device_id_type=MESH
        )
    own = groups - 1
    smalls[0].wait()
    smalls[1].wait()
    gath[own, :, 0:depth] = down_v[...]
    gath[own, :, depth : depth + cols] = up_v[...]
    gath[own, :, depth + cols :] = jnp.zeros(
        (gath.shape[1], gath.shape[2] - depth - cols), gath.dtype
    )
    pl.semaphore_wait(barrier, (groups - 1) + 1 + (chips - 1))

    def send_factors(d, carry):
        pltpu.make_async_remote_copy(
            src_ref=gath.at[own],
            dst_ref=gath.at[d],
            send_sem=gsend_sem,
            recv_sem=grecv_sem,
            device_id={"group": lax.rem(g + d + 1, groups)},
            device_id_type=MESH,
        ).start()
        return carry

    lax.fori_loop(0, groups - 1, send_factors, 0)

    for c in smalls[2:]:
        c.wait()
    q32 = jnp.concatenate([q_v[s].astype(jnp.float32) for s in range(steps)], axis=0)
    q64 = jnp.concatenate([q32[:, h * HEAD_SIZE : (h + 1) * HEAD_SIZE] for h in range(QH)], axis=0)
    height = QH * toks
    row_of = lax.broadcasted_iota(jnp.int32, (height, 1), 0) % rows
    step_of = (lax.broadcasted_iota(jnp.int32, (height, 1), 0) // rows) % steps
    q_wide = jnp.concatenate(
        [jnp.where(row_of == r, q64, 0.0).astype(jnp.bfloat16) for r in range(rows)], axis=1
    )
    sk = jnp.concatenate([sk_v[s].astype(jnp.float32) for s in range(steps)], axis=0)
    sv = jnp.concatenate([sv_v[s].astype(jnp.float32) for s in range(steps)], axis=0)
    recent = nt_dot(q64.astype(jnp.bfloat16), sk.astype(jnp.bfloat16))
    col = lax.broadcasted_iota(jnp.int32, (height, toks), 1)
    recent = jnp.where((col % rows == row_of) & (col // rows <= step_of), recent, NEG)
    lane = lax.broadcasted_iota(jnp.int32, (rows, rows), 1)
    sub = lax.broadcasted_iota(jnp.int32, (rows, rows), 0)
    lens = jnp.sum(
        jnp.where(lane == sub, jnp.broadcast_to(len_v[...], (rows, rows)), 0).astype(jnp.float32),
        axis=1,
        keepdims=True,
    )
    lens = jnp.concatenate([lens] * (QH * steps), axis=0)
    for c in k_copies:
        c.wait()
    cached = nt_dot(q_wide, k_v[...])
    position = lax.broadcasted_iota(jnp.int32, (height, cache), 1).astype(jnp.float32)
    cached = jnp.where(position < lens, cached, NEG)
    top = jnp.maximum(
        jnp.max(cached, axis=1, keepdims=True), jnp.max(recent, axis=1, keepdims=True)
    )
    cached = jnp.exp2((cached - top) * EXP2_SCALE)
    recent = jnp.exp2((recent - top) * EXP2_SCALE)
    norm = 1.0 / (
        jnp.sum(cached, axis=1, keepdims=True) + jnp.sum(recent, axis=1, keepdims=True)
    )
    cached = cached * norm
    recent = (recent * norm).astype(jnp.bfloat16)
    for c in v_copies:
        c.wait()
    mixed = jnp.dot(recent, sv.astype(jnp.bfloat16), preferred_element_type=jnp.float32)
    weights = jnp.concatenate(
        [jnp.where(row_of == r, cached, 0.0).astype(jnp.bfloat16) for r in range(rows)], axis=1
    )
    mixed = mixed + jnp.dot(weights, v_v[...], preferred_element_type=jnp.float32)
    attended = jnp.concatenate([mixed[h * toks : (h + 1) * toks] for h in range(QH)], axis=1)
    attended = attended.astype(jnp.bfloat16)

    others = gath.at[pl.ds(0, groups - 1)]
    pltpu.make_async_copy(others, others, grecv_sem).wait()
    per = gath.shape[1]
    for i in range(groups):
        factors[per * i : per * (i + 1), :] = gath[i].astype(jnp.float32)
    low = nt_dot(attended, factors[:, 0:depth].astype(jnp.bfloat16))

    to_partner = []
    for k in range(chips):
        w_copies[k].wait()
        part = jnp.dot(attended, w_v[k], preferred_element_type=jnp.float32)
        first, second = part[:, :cols], part[:, cols:]
        mine = jnp.where(core == 0, first, second)
        theirs = jnp.where(core == 0, second, first)
        keep[k, :, :] = jnp.concatenate([mine, low], axis=1)
        send1[k, :, :] = jnp.concatenate([theirs, low], axis=1).astype(jnp.bfloat16)
        copy = pltpu.make_async_remote_copy(
            src_ref=send1.at[k],
            dst_ref=recv1.at[k],
            send_sem=s1_sem.at[k],
            recv_sem=r1_sem.at[k],
            device_id={"tensor": t + 1 - 2 * core},
            device_id_type=MESH,
        )
        copy.start()
        to_partner.append(copy)

    to_chips = []
    for k in range(chips):
        to_partner[k].wait_recv()
        both = keep[k] + recv1[k].astype(jnp.float32)
        if k < chips - 1:
            send2[k, :, :] = both.astype(jnp.bfloat16)
            copy = pltpu.make_async_remote_copy(
                src_ref=send2.at[k],
                dst_ref=recv2.at[k],
                send_sem=s2_sem.at[k],
                recv_sem=r2_sem.at[k],
                device_id={"tensor": chunk_at(k) * 2 + core},
                device_id_type=MESH,
            )
            copy.start()
            to_chips.append(copy)
        else:
            total = both

    up = factors[:, depth : depth + cols].astype(jnp.bfloat16)
    for k in range(chips - 1):
        to_chips[k].wait_recv()
        total = total + recv2[k].astype(jnp.float32)
    low = total[:, cols : cols + rank]
    high = low.astype(jnp.bfloat16)
    rest = (low - high.astype(jnp.float32)).astype(jnp.bfloat16)
    delta = jnp.dot(high, up, preferred_element_type=jnp.float32) + jnp.dot(
        rest, up, preferred_element_type=jnp.float32
    )
    result = (total[:, :cols] + 2.0 * delta).astype(out_ref.dtype)
    for s in range(steps):
        out_ref[s, :, :] = result[s * rows : (s + 1) * rows]

    pltpu.make_async_copy(others, others, gsend_sem).wait()
    for copy in to_partner + to_chips:
        copy.wait_send()


def on_device(mesh_shape, queries, keys, values, step_keys, step_values, lengths, weight, down, up):
    groups, tensors = mesh_shape
    steps, rows, width = queries.shape
    cache = keys.shape[2]
    depth, per = down.shape
    cols = up.shape[1]
    chips = tensors // 2
    toks = steps * rows
    rank = per * groups
    chunk = cols + rank
    message = -(-(depth + cols) // 128) * 128
    bf16, f32 = jnp.bfloat16, jnp.float32
    hbm = pl.BlockSpec(memory_space=pltpu.HBM)
    dma = pltpu.SemaphoreType.DMA
    return pl.pallas_call(
        functools.partial(kernel, groups, tensors),
        out_shape=jax.ShapeDtypeStruct((steps, rows, cols), bf16),
        in_specs=[hbm] * 9,
        out_specs=pl.BlockSpec(memory_space=pltpu.VMEM),
        scratch_shapes=[
            pltpu.VMEM((steps, rows, width), bf16),
            pltpu.VMEM((cache, rows * HEAD_SIZE), bf16),
            pltpu.VMEM((rows * cache, HEAD_SIZE), bf16),
            pltpu.VMEM((steps, rows, HEAD_SIZE), bf16),
            pltpu.VMEM((steps, rows, HEAD_SIZE), bf16),
            pltpu.VMEM((1, rows), jnp.int32),
            pltpu.VMEM((chips, depth, 2 * cols), bf16),
            pltpu.VMEM((per, depth), bf16),
            pltpu.VMEM((per, cols), bf16),
            pltpu.VMEM((groups, per, message), bf16),
            pltpu.VMEM((rank, message), f32),
            pltpu.VMEM((chips, toks, chunk), f32),
            pltpu.VMEM((chips, toks, chunk), bf16),
            pltpu.VMEM((chips, toks, chunk), bf16),
            pltpu.VMEM((chips - 1, toks, chunk), bf16),
            pltpu.VMEM((chips - 1, toks, chunk), bf16),
            dma((6,)),
            dma((rows,)),
            dma((rows,)),
            dma((chips,)),
            dma,
            dma,
            dma((chips,)),
            dma((chips,)),
            dma((chips - 1,)),
            dma((chips - 1,)),
        ],
        compiler_params=pltpu.CompilerParams(
            collective_id=0, has_side_effects=True, vmem_limit_bytes=VMEM_BYTES
        ),
    )(
        queries,
        keys[:, 0],
        values[:, 0],
        step_keys[:, :, 0],
        step_values[:, :, 0],
        lengths[None, :],
        weight,
        down.T,
        up,
    )


def solution(mesh):
    return jax.shard_map(
        functools.partial(on_device, (mesh.shape["group"], mesh.shape["tensor"])),
        mesh=mesh,
        in_specs=(
            P(None, "group", "tensor"),
            P("group", "tensor", None, None),
            P("group", "tensor", None, None),
            P(None, "group", "tensor", None),
            P(None, "group", "tensor", None),
            P("group"),
            P("tensor", None),
            P("tensor", "group"),
            P("group", "tensor"),
        ),
        out_specs=P(None, "group", "tensor"),
        check_vma=False,
    )
```

```python
import functools
import math

import jax
import jax.numpy as jnp
from jax import lax
from jax.experimental import pallas as pl
from jax.experimental.pallas import tpu as pltpu
from jax.sharding import PartitionSpec as P

MESH = pl.DeviceIdType.MESH
HEAD_SIZE = 128
QH = 2
EXP2_SCALE = HEAD_SIZE**-0.5 / math.log(2.0)
NEG = -1e30
VMEM_BYTES = 63 * 1024 * 1024


def nt_dot(a, b):
    return lax.dot_general(a, b, (((1,), (1,)), ((), ())), preferred_element_type=jnp.float32)


def kernel(
    groups,
    tensors,
    q_hbm,
    k_hbm,
    v_hbm,
    sk_hbm,
    sv_hbm,
    len_hbm,
    w_hbm,
    down_hbm,
    up_hbm,
    out_ref,
    q_v,
    k_v,
    v_v,
    sk_v,
    sv_v,
    len_v,
    w_v,
    down_v,
    up_v,
    gath,
    down_f,
    up_f,
    lows,
    keep,
    send1,
    recv1,
    send2,
    recv2,
    small_sem,
    k_sem,
    v_sem,
    w_sem,
    met_sem,
    mine_sem,
    gath_sent,
    gath_sem,
    low_sent,
    low_sem,
    s1_sem,
    r1_sem,
    s2_sem,
    r2_sem,
):
    steps, rows, _ = q_v.shape
    cache = k_v.shape[0]
    toks = steps * rows
    cols = out_ref.shape[2]
    chips = tensors // 2
    rank = down_f.shape[0]

    g = lax.axis_index("group")
    t = lax.axis_index("tensor")
    chip = t // 2
    core = t % 2
    planes = groups // 2
    z = lax.rem(g, planes)
    order = 2 * z + g // planes
    late = (2 * z) // planes

    smalls = [
        pltpu.make_async_copy(src, dst, small_sem.at[i])
        for i, (src, dst) in enumerate(
            [
                (q_hbm, q_v),
                (sk_hbm, sk_v),
                (sv_hbm, sv_v),
                (len_hbm, len_v),
            ]
        )
    ]
    k_copies = [
        pltpu.make_async_copy(k_hbm.at[r], k_v.at[:, pl.ds(r * HEAD_SIZE, HEAD_SIZE)], k_sem.at[r])
        for r in range(rows)
    ]
    v_copies = [
        pltpu.make_async_copy(v_hbm.at[r], v_v.at[pl.ds(r * cache, cache)], v_sem.at[r])
        for r in range(rows)
    ]
    pair = 2 * cols

    def chunk_at(k):
        return lax.rem(chip + k + 1, chips)

    w_copies = [
        pltpu.make_async_copy(
            w_hbm.at[:, pl.ds(pl.multiple_of(chunk_at(k) * pair, 128), pair)], w_v.at[k], w_sem.at[k]
        )
        for k in range(chips)
    ]
    mine_copies = [
        pltpu.make_async_copy(down_hbm, down_v, mine_sem.at[0]),
        pltpu.make_async_copy(up_hbm, up_v, mine_sem.at[1]),
    ]
    for c in mine_copies + smalls + k_copies + v_copies + w_copies:
        c.start()

    barrier = pltpu.get_barrier_semaphore()
    home = t - core
    partner = {"tensor": home + 1 - core}

    def group_at(k):
        return lax.rem(k, 2) * planes + k // 2

    def greet_group(k, carry):
        pl.semaphore_signal(
            barrier,
            inc=1,
            device_id={"group": group_at(k), "tensor": home + late},
            device_id_type=MESH,
        )
        return carry

    lax.fori_loop(0, order, greet_group, 0)
    lax.fori_loop(order + 1, groups, greet_group, 0)
    for k in range(chips - 1):
        pl.semaphore_signal(
            barrier, inc=1, device_id={"tensor": chunk_at(k) * 2 + late}, device_id_type=MESH
        )

    @pl.when(core == 1)
    def _():
        pl.semaphore_signal(barrier, inc=1, device_id=partner, device_id_type=MESH)

    for c in mine_copies:
        c.wait()
    depth = down_v.shape[1]
    gath[order, :, 0:depth] = down_v[...]
    gath[order, :, depth : depth + cols] = up_v[...]
    gath[order, :, depth + cols :] = jnp.zeros(
        (gath.shape[1], gath.shape[2] - depth - cols), gath.dtype
    )

    def send_factors(k, carry):
        pltpu.make_async_remote_copy(
            src_ref=gath.at[order],
            dst_ref=gath.at[order],
            send_sem=gath_sent,
            recv_sem=gath_sem,
            device_id={"group": group_at(k)},
            device_id_type=MESH,
        ).start()
        return carry

    half = groups // 2

    def meet(mail, count, first):
        @pl.when(core == mail)
        def _():
            pl.semaphore_wait(barrier, count)
            pl.semaphore_signal(met_sem.at[mail], inc=1, device_id=partner, device_id_type=MESH)

        @pl.when(core != mail)
        def _():
            pl.semaphore_wait(met_sem.at[mail], 1)

        lax.fori_loop(first, jnp.clip(order, first, first + half), send_factors, 0)
        lax.fori_loop(jnp.clip(order + 1, first, first + half), first + half, send_factors, 0)

    plane = 2 * (chips - 1)

    def meet_first():
        meet(0, 2 * half + 1 + (1 - late) * (plane - 2), 0)

    def meet_second():
        meet(1, 2 * half + late * (plane - 2), half)

    hurry = 4 * z >= planes
    pl.when(hurry)(meet_first)

    for c in smalls:
        c.wait()
    q32 = jnp.concatenate([q_v[s].astype(jnp.float32) for s in range(steps)], axis=0)
    q64 = jnp.concatenate([q32[:, h * HEAD_SIZE : (h + 1) * HEAD_SIZE] for h in range(QH)], axis=0)
    height = QH * toks
    row_of = lax.broadcasted_iota(jnp.int32, (height, 1), 0) % rows
    step_of = (lax.broadcasted_iota(jnp.int32, (height, 1), 0) // rows) % steps
    q_wide = jnp.concatenate(
        [jnp.where(row_of == r, q64, 0.0).astype(jnp.bfloat16) for r in range(rows)], axis=1
    )
    sk = jnp.concatenate([sk_v[s].astype(jnp.float32) for s in range(steps)], axis=0)
    sv = jnp.concatenate([sv_v[s].astype(jnp.float32) for s in range(steps)], axis=0)
    recent = nt_dot(q64.astype(jnp.bfloat16), sk.astype(jnp.bfloat16))
    col = lax.broadcasted_iota(jnp.int32, (height, toks), 1)
    recent = jnp.where((col % rows == row_of) & (col // rows <= step_of), recent, NEG)
    lane = lax.broadcasted_iota(jnp.int32, (rows, rows), 1)
    sub = lax.broadcasted_iota(jnp.int32, (rows, rows), 0)
    lens = jnp.sum(
        jnp.where(lane == sub, jnp.broadcast_to(len_v[...], (rows, rows)), 0).astype(jnp.float32),
        axis=1,
        keepdims=True,
    )
    lens = jnp.concatenate([lens] * (QH * steps), axis=0)
    for c in k_copies:
        c.wait()
    cached = nt_dot(q_wide, k_v[...])
    position = lax.broadcasted_iota(jnp.int32, (height, cache), 1).astype(jnp.float32)
    cached = jnp.where(position < lens, cached, NEG)
    top = jnp.maximum(
        jnp.max(cached, axis=1, keepdims=True), jnp.max(recent, axis=1, keepdims=True)
    )
    cached = jnp.exp2((cached - top) * EXP2_SCALE)
    recent = jnp.exp2((recent - top) * EXP2_SCALE)
    norm = 1.0 / (
        jnp.sum(cached, axis=1, keepdims=True) + jnp.sum(recent, axis=1, keepdims=True)
    )
    cached = cached * norm
    recent = (recent * norm).astype(jnp.bfloat16)
    for c in v_copies:
        c.wait()
    mixed = jnp.dot(recent, sv.astype(jnp.bfloat16), preferred_element_type=jnp.float32)
    weights = jnp.concatenate(
        [jnp.where(row_of == r, cached, 0.0).astype(jnp.bfloat16) for r in range(rows)], axis=1
    )
    mixed = mixed + jnp.dot(weights, v_v[...], preferred_element_type=jnp.float32)
    attended = jnp.concatenate([mixed[h * toks : (h + 1) * toks] for h in range(QH)], axis=1)
    attended = attended.astype(jnp.bfloat16)

    for k in range(chips):
        w_copies[k].wait()
        part = jnp.dot(attended, w_v[k], preferred_element_type=jnp.float32)
        first, second = part[:, :cols], part[:, cols:]
        keep[k, :, :] = jnp.where(core == 0, first, second)
        send1[k, :, :] = jnp.where(core == 0, second, first).astype(jnp.bfloat16)

    pl.when(jnp.logical_not(hurry))(meet_first)
    pl.when(late == 1)(meet_second)

    to_partner = []
    for k in range(chips):
        copy = pltpu.make_async_remote_copy(
            src_ref=send1.at[k],
            dst_ref=recv1.at[k],
            send_sem=s1_sem.at[k],
            recv_sem=r1_sem.at[k],
            device_id={"tensor": t + 1 - 2 * core},
            device_id_type=MESH,
        )
        copy.start()
        to_partner.append(copy)

    to_chips = []
    for k in range(chips):
        to_partner[k].wait_recv()
        both = keep[k] + recv1[k].astype(jnp.float32)
        if k < chips - 1:
            send2[k, :, :] = both.astype(jnp.bfloat16)
            copy = pltpu.make_async_remote_copy(
                src_ref=send2.at[k],
                dst_ref=recv2.at[k],
                send_sem=s2_sem.at[k],
                recv_sem=r2_sem.at[k],
                device_id={"tensor": chunk_at(k) * 2 + core},
                device_id_type=MESH,
            )
            copy.start()
            to_chips.append(copy)
        else:
            total = both

    pl.when(late == 0)(meet_second)
    others = gath.at[pl.ds(0, groups - 1)]
    pltpu.make_async_copy(others, others, gath_sem).wait()

    per = gath.shape[1]
    for i in range(groups):
        down_f[per * i : per * (i + 1), :] = gath[i, :, 0:depth].astype(jnp.float32)
    low = nt_dot(attended, down_f[...].astype(jnp.bfloat16))
    top_rows = toks // 2
    low = jnp.concatenate([low[:top_rows], low[top_rows:]], axis=1)
    lows[tensors - 1, :, :] = low.astype(jnp.bfloat16)
    low_copies = [
        pltpu.make_async_remote_copy(
            src_ref=lows.at[tensors - 1],
            dst_ref=lows.at[d],
            send_sem=low_sent,
            recv_sem=low_sem,
            device_id={"tensor": lax.rem(t + d + 1, tensors)},
            device_id_type=MESH,
        )
        for d in range(tensors - 1)
    ]
    for copy in low_copies:
        copy.start()

    for i in range(groups):
        up_f[per * i : per * (i + 1), :] = gath[i, :, depth : depth + cols].astype(jnp.float32)
    up = up_f[...].astype(jnp.bfloat16)
    up = jnp.concatenate([up, up], axis=0)
    for k in range(chips - 1):
        to_chips[k].wait_recv()
        total = total + recv2[k].astype(jnp.float32)
    others = lows.at[pl.ds(0, tensors - 1)]
    pltpu.make_async_copy(others, others, low_sem).wait()
    low = lows[0].astype(jnp.float32)
    for d in range(1, tensors):
        low = low + lows[d].astype(jnp.float32)
    left = lax.broadcasted_iota(jnp.int32, low.shape, 1) < rank
    low = jnp.concatenate([jnp.where(left, low, 0.0), jnp.where(left, 0.0, low)], axis=0)
    high = low.astype(jnp.bfloat16)
    rest = (low - high.astype(jnp.float32)).astype(jnp.bfloat16)
    delta = jnp.dot(high, up, preferred_element_type=jnp.float32) + jnp.dot(
        rest, up, preferred_element_type=jnp.float32
    )
    result = (total + 2.0 * delta).astype(out_ref.dtype)
    for s in range(steps):
        out_ref[s, :, :] = result[s * rows : (s + 1) * rows]

    pltpu.make_async_copy(others, others, low_sent).wait()
    others = gath.at[pl.ds(0, groups - 1)]
    pltpu.make_async_copy(others, others, gath_sent).wait()
    for copy in to_partner + to_chips:
        copy.wait_send()


def on_device(mesh_shape, queries, keys, values, step_keys, step_values, lengths, weight, down, up):
    groups, tensors = mesh_shape
    steps, rows, width = queries.shape
    cache = keys.shape[2]
    depth, per = down.shape
    cols = up.shape[1]
    chips = tensors // 2
    toks = steps * rows
    rank = per * groups
    message = -(-(depth + cols) // 128) * 128
    bf16, f32 = jnp.bfloat16, jnp.float32
    hbm = pl.BlockSpec(memory_space=pltpu.HBM)
    dma = pltpu.SemaphoreType.DMA
    return pl.pallas_call(
        functools.partial(kernel, groups, tensors),
        out_shape=jax.ShapeDtypeStruct((steps, rows, cols), bf16),
        in_specs=[hbm] * 9,
        out_specs=pl.BlockSpec(memory_space=pltpu.VMEM),
        scratch_shapes=[
            pltpu.VMEM((steps, rows, width), bf16),
            pltpu.VMEM((cache, rows * HEAD_SIZE), bf16),
            pltpu.VMEM((rows * cache, HEAD_SIZE), bf16),
            pltpu.VMEM((steps, rows, HEAD_SIZE), bf16),
            pltpu.VMEM((steps, rows, HEAD_SIZE), bf16),
            pltpu.VMEM((1, rows), jnp.int32),
            pltpu.VMEM((chips, depth, 2 * cols), bf16),
            pltpu.VMEM((per, depth), bf16),
            pltpu.VMEM((per, cols), bf16),
            pltpu.VMEM((groups, per, message), bf16),
            pltpu.VMEM((rank, depth), f32),
            pltpu.VMEM((rank, cols), f32),
            pltpu.VMEM((tensors, toks // 2, 2 * rank), bf16),
            pltpu.VMEM((chips, toks, cols), f32),
            pltpu.VMEM((chips, toks, cols), bf16),
            pltpu.VMEM((chips, toks, cols), bf16),
            pltpu.VMEM((chips - 1, toks, cols), bf16),
            pltpu.VMEM((chips - 1, toks, cols), bf16),
            dma((4,)),
            dma((rows,)),
            dma((rows,)),
            dma((chips,)),
            pltpu.SemaphoreType.REGULAR((2,)),
            dma((2,)),
            dma,
            dma,
            dma,
            dma,
            dma((chips,)),
            dma((chips,)),
            dma((chips - 1,)),
            dma((chips - 1,)),
        ],
        compiler_params=pltpu.CompilerParams(
            collective_id=0, has_side_effects=True, vmem_limit_bytes=VMEM_BYTES
        ),
    )(
        queries,
        keys[:, 0],
        values[:, 0],
        step_keys[:, :, 0],
        step_values[:, :, 0],
        lengths[None, :],
        weight,
        down.T,
        up,
    )


def solution(mesh):
    return jax.shard_map(
        functools.partial(on_device, (mesh.shape["group"], mesh.shape["tensor"])),
        mesh=mesh,
        in_specs=(
            P(None, "group", "tensor"),
            P("group", "tensor", None, None),
            P("group", "tensor", None, None),
            P(None, "group", "tensor", None),
            P(None, "group", "tensor", None),
            P("group"),
            P("tensor", None),
            P("tensor", "group"),
            P("group", "tensor"),
        ),
        out_specs=P(None, "group", "tensor"),
        check_vma=False,
    )
```

```python
import functools
import math

import jax
import jax.numpy as jnp
from jax import lax
from jax.experimental import pallas as pl
from jax.experimental.pallas import tpu as pltpu
from jax.sharding import PartitionSpec as P

MESH = pl.DeviceIdType.MESH
HEAD_SIZE = 128
QH = 2
EXP2_SCALE = HEAD_SIZE**-0.5 / math.log(2.0)
NEG = -1e30
VMEM_BYTES = 63 * 1024 * 1024


def nt_dot(a, b):
    return lax.dot_general(a, b, (((1,), (1,)), ((), ())), preferred_element_type=jnp.float32)


def kernel(
    groups,
    tensors,
    q_hbm,
    k_hbm,
    v_hbm,
    sk_hbm,
    sv_hbm,
    len_hbm,
    w_hbm,
    down_hbm,
    up_hbm,
    out_ref,
    q_v,
    k_v,
    v_v,
    sk_v,
    sv_v,
    len_v,
    w_v,
    down_v,
    up_v,
    gdown,
    gup,
    down_f,
    up_f,
    lows,
    keep,
    send1,
    recv1,
    send2,
    recv2,
    small_sem,
    k_sem,
    v_sem,
    w_sem,
    met_sem,
    mine_sem,
    sent_sem,
    come_sem,
    low_sent,
    low_sem,
    s1_sem,
    r1_sem,
    s2_sem,
    r2_sem,
):
    steps, rows, _ = q_v.shape
    cache = k_v.shape[0]
    toks = steps * rows
    cols = out_ref.shape[2]
    chips = tensors // 2
    rank = down_f.shape[0]

    g = lax.axis_index("group")
    t = lax.axis_index("tensor")
    chip = t // 2
    core = t % 2
    planes = groups // 2
    z = lax.rem(g, planes)
    order = 2 * z + g // planes
    late = (2 * z) // planes

    smalls = [
        pltpu.make_async_copy(src, dst, small_sem.at[i])
        for i, (src, dst) in enumerate(
            [
                (q_hbm, q_v),
                (sk_hbm, sk_v),
                (sv_hbm, sv_v),
                (len_hbm, len_v),
            ]
        )
    ]
    k_copies = [
        pltpu.make_async_copy(k_hbm.at[r], k_v.at[:, pl.ds(r * HEAD_SIZE, HEAD_SIZE)], k_sem.at[r])
        for r in range(rows)
    ]
    v_copies = [
        pltpu.make_async_copy(v_hbm.at[r], v_v.at[pl.ds(r * cache, cache)], v_sem.at[r])
        for r in range(rows)
    ]
    pair = 2 * cols

    def chunk_at(k):
        return lax.rem(chip + k + 1, chips)

    w_copies = [
        pltpu.make_async_copy(
            w_hbm.at[:, pl.ds(pl.multiple_of(chunk_at(k) * pair, 128), pair)], w_v.at[k], w_sem.at[k]
        )
        for k in range(chips)
    ]
    mine_copies = [
        pltpu.make_async_copy(down_hbm, down_v, mine_sem.at[0]),
        pltpu.make_async_copy(up_hbm, up_v, mine_sem.at[1]),
    ]
    for c in mine_copies:
        c.start()

    def start_loads():
        for c in smalls + k_copies + v_copies + w_copies:
            c.start()


    barrier = pltpu.get_barrier_semaphore()
    home = t - core
    partner = {"tensor": home + 1 - core}
    half = groups // 2
    first_mail = 0
    plane = 2 * (chips - 1)

    @pl.when(core != first_mail)
    def _():
        pl.semaphore_signal(barrier, inc=1, device_id=partner, device_id_type=MESH)

    def group_at(k):
        return lax.rem(k, 2) * planes + k // 2

    def greet():
        def greet_group(i, carry):
            away = (i + 1) // 2 * (1 - 2 * lax.rem(i, 2))
            k = lax.rem(order + half + away + groups, groups)
            there = k // half
            mail = late
            pl.semaphore_signal(
                barrier,
                inc=1,
                device_id={"group": group_at(k), "tensor": home + mail},
                device_id_type=MESH,
            )
            return carry

        lax.fori_loop(0, groups - 1, greet_group, 0)
        for k in range(chips - 1):
            pl.semaphore_signal(
                barrier, inc=1, device_id={"tensor": chunk_at(k) * 2 + late}, device_id_type=MESH
            )

    def meet(which, mail, count):
        @pl.when(core == mail)
        def _():
            pl.semaphore_wait(barrier, count)
            pl.semaphore_signal(met_sem.at[which], inc=1, device_id=partner, device_id_type=MESH)

        @pl.when(core != mail)
        def _():
            pl.semaphore_wait(met_sem.at[which], 1)

    def meet_first():
        meet(0, first_mail, 2 * half + 1 + (1 - late) * (plane - 2))

    def meet_second():
        meet(1, 1 - first_mail, 2 * half + late * (plane - 2))

    def send_to(first, which):
        src, dst = ((down_v, gdown), (up_v, gup))[which]

        def send(k, carry):
            pltpu.make_async_remote_copy(
                src_ref=src,
                dst_ref=dst.at[order],
                send_sem=sent_sem.at[which],
                recv_sem=come_sem.at[which],
                device_id={"group": group_at(k)},
                device_id_type=MESH,
            ).start()
            return carry

        lax.fori_loop(first, jnp.clip(order, first, first + half), send, 0)
        lax.fori_loop(jnp.clip(order + 1, first, first + half), first + half, send, 0)

    def wait_mine():
        for c in mine_copies:
            c.wait()

    hurry = 4 * z >= planes

    greet()
    start_loads()
    wait_mine()

    @pl.when(hurry)
    def _():
        meet_first()
        send_to(0, 0)

    for c in smalls:
        c.wait()
    q32 = jnp.concatenate([q_v[s].astype(jnp.float32) for s in range(steps)], axis=0)
    q64 = jnp.concatenate([q32[:, h * HEAD_SIZE : (h + 1) * HEAD_SIZE] for h in range(QH)], axis=0)
    height = QH * toks
    row_of = lax.broadcasted_iota(jnp.int32, (height, 1), 0) % rows
    step_of = (lax.broadcasted_iota(jnp.int32, (height, 1), 0) // rows) % steps
    q_wide = jnp.concatenate(
        [jnp.where(row_of == r, q64, 0.0).astype(jnp.bfloat16) for r in range(rows)], axis=1
    )
    sk = jnp.concatenate([sk_v[s].astype(jnp.float32) for s in range(steps)], axis=0)
    sv = jnp.concatenate([sv_v[s].astype(jnp.float32) for s in range(steps)], axis=0)
    recent = nt_dot(q64.astype(jnp.bfloat16), sk.astype(jnp.bfloat16))
    col = lax.broadcasted_iota(jnp.int32, (height, toks), 1)
    recent = jnp.where((col % rows == row_of) & (col // rows <= step_of), recent, NEG)
    lane = lax.broadcasted_iota(jnp.int32, (rows, rows), 1)
    sub = lax.broadcasted_iota(jnp.int32, (rows, rows), 0)
    lens = jnp.sum(
        jnp.where(lane == sub, jnp.broadcast_to(len_v[...], (rows, rows)), 0).astype(jnp.float32),
        axis=1,
        keepdims=True,
    )
    lens = jnp.concatenate([lens] * (QH * steps), axis=0)
    for c in k_copies:
        c.wait()
    cached = nt_dot(q_wide, k_v[...])
    position = lax.broadcasted_iota(jnp.int32, (height, cache), 1).astype(jnp.float32)
    cached = jnp.where(position < lens, cached, NEG)
    top = jnp.maximum(
        jnp.max(cached, axis=1, keepdims=True), jnp.max(recent, axis=1, keepdims=True)
    )
    cached = jnp.exp2((cached - top) * EXP2_SCALE)
    recent = jnp.exp2((recent - top) * EXP2_SCALE)
    norm = 1.0 / (
        jnp.sum(cached, axis=1, keepdims=True) + jnp.sum(recent, axis=1, keepdims=True)
    )
    cached = cached * norm
    recent = (recent * norm).astype(jnp.bfloat16)
    for c in v_copies:
        c.wait()
    mixed = jnp.dot(recent, sv.astype(jnp.bfloat16), preferred_element_type=jnp.float32)
    weights = jnp.concatenate(
        [jnp.where(row_of == r, cached, 0.0).astype(jnp.bfloat16) for r in range(rows)], axis=1
    )
    mixed = mixed + jnp.dot(weights, v_v[...], preferred_element_type=jnp.float32)
    attended = jnp.concatenate([mixed[h * toks : (h + 1) * toks] for h in range(QH)], axis=1)
    attended = attended.astype(jnp.bfloat16)

    pl.when(hurry)(lambda: send_to(0, 1))

    for k in range(chips):
        w_copies[k].wait()
        part = jnp.dot(attended, w_v[k], preferred_element_type=jnp.float32)
        first, second = part[:, :cols], part[:, cols:]
        keep[k, :, :] = jnp.where(core == 0, first, second)
        send1[k, :, :] = jnp.where(core == 0, second, first).astype(jnp.bfloat16)

    @pl.when(jnp.logical_not(hurry))
    def _():
        meet_first()
        send_to(0, 0)
        send_to(0, 1)

    @pl.when(late == 1)
    def _():
        meet_second()
        send_to(half, 0)


    to_partner = []
    for k in range(chips):
        copy = pltpu.make_async_remote_copy(
            src_ref=send1.at[k],
            dst_ref=recv1.at[k],
            send_sem=s1_sem.at[k],
            recv_sem=r1_sem.at[k],
            device_id={"tensor": t + 1 - 2 * core},
            device_id_type=MESH,
        )
        copy.start()
        to_partner.append(copy)

    to_chips = []
    for k in range(chips):
        to_partner[k].wait_recv()
        both = keep[k] + recv1[k].astype(jnp.float32)
        if k < chips - 1:
            send2[k, :, :] = both.astype(jnp.bfloat16)
            copy = pltpu.make_async_remote_copy(
                src_ref=send2.at[k],
                dst_ref=recv2.at[k],
                send_sem=s2_sem.at[k],
                recv_sem=r2_sem.at[k],
                device_id={"tensor": chunk_at(k) * 2 + core},
                device_id_type=MESH,
            )
            copy.start()
            to_chips.append(copy)
        else:
            total = both

    @pl.when(late == 0)
    def _():
        meet_second()
        send_to(half, 0)

    gdown[order] = down_v[...]
    gup[order] = up_v[...]
    downs = gdown.at[pl.ds(0, groups - 1)]
    ups = gup.at[pl.ds(0, groups - 1)]
    pltpu.make_async_copy(downs, downs, come_sem.at[0]).wait()

    per = gdown.shape[1]
    for i in range(groups):
        down_f[per * i : per * (i + 1), :] = gdown[i].astype(jnp.float32)
    low = nt_dot(attended, down_f[...].astype(jnp.bfloat16))
    top_rows = toks // 2
    low = jnp.concatenate([low[:top_rows], low[top_rows:]], axis=1)
    lows[tensors - 1, :, :] = low.astype(jnp.bfloat16)
    low_copies = [
        pltpu.make_async_remote_copy(
            src_ref=lows.at[tensors - 1],
            dst_ref=lows.at[d],
            send_sem=low_sent,
            recv_sem=low_sem,
            device_id={"tensor": lax.rem(t + d + 1, tensors)},
            device_id_type=MESH,
        )
        for d in range(tensors - 1)
    ]
    for copy in low_copies:
        copy.start()

    send_to(half, 1)
    pltpu.make_async_copy(ups, ups, come_sem.at[1]).wait()
    for i in range(groups):
        up_f[per * i : per * (i + 1), :] = gup[i].astype(jnp.float32)
    up = up_f[...].astype(jnp.bfloat16)
    up = jnp.concatenate([up, up], axis=0)
    for k in range(chips - 1):
        to_chips[k].wait_recv()
        total = total + recv2[k].astype(jnp.float32)
    others = lows.at[pl.ds(0, tensors - 1)]
    pltpu.make_async_copy(others, others, low_sem).wait()
    low = lows[0].astype(jnp.float32)
    for d in range(1, tensors):
        low = low + lows[d].astype(jnp.float32)
    left = lax.broadcasted_iota(jnp.int32, low.shape, 1) < rank
    low = jnp.concatenate([jnp.where(left, low, 0.0), jnp.where(left, 0.0, low)], axis=0)
    high = low.astype(jnp.bfloat16)
    rest = (low - high.astype(jnp.float32)).astype(jnp.bfloat16)
    delta = jnp.dot(high, up, preferred_element_type=jnp.float32) + jnp.dot(
        rest, up, preferred_element_type=jnp.float32
    )
    result = (total + 2.0 * delta).astype(out_ref.dtype)
    for s in range(steps):
        out_ref[s, :, :] = result[s * rows : (s + 1) * rows]

    pltpu.make_async_copy(others, others, low_sent).wait()
    pltpu.make_async_copy(downs, downs, sent_sem.at[0]).wait()
    pltpu.make_async_copy(ups, ups, sent_sem.at[1]).wait()
    for copy in to_partner + to_chips:
        copy.wait_send()


def on_device(mesh_shape, queries, keys, values, step_keys, step_values, lengths, weight, down, up):
    groups, tensors = mesh_shape
    steps, rows, width = queries.shape
    cache = keys.shape[2]
    depth, per = down.shape
    cols = up.shape[1]
    chips = tensors // 2
    toks = steps * rows
    rank = per * groups
    bf16, f32 = jnp.bfloat16, jnp.float32
    hbm = pl.BlockSpec(memory_space=pltpu.HBM)
    dma = pltpu.SemaphoreType.DMA
    return pl.pallas_call(
        functools.partial(kernel, groups, tensors),
        out_shape=pltpu.VMEM((steps, rows, cols), bf16),
        in_specs=[hbm] * 9,
        out_specs=pl.BlockSpec(memory_space=pltpu.VMEM),
        scratch_shapes=[
            pltpu.VMEM((steps, rows, width), bf16),
            pltpu.VMEM((cache, rows * HEAD_SIZE), bf16),
            pltpu.VMEM((rows * cache, HEAD_SIZE), bf16),
            pltpu.VMEM((steps, rows, HEAD_SIZE), bf16),
            pltpu.VMEM((steps, rows, HEAD_SIZE), bf16),
            pltpu.VMEM((1, rows), jnp.int32),
            pltpu.VMEM((chips, depth, 2 * cols), bf16),
            pltpu.VMEM((per, depth), bf16),
            pltpu.VMEM((per, cols), bf16),
            pltpu.VMEM((groups, per, depth), bf16),
            pltpu.VMEM((groups, per, cols), bf16),
            pltpu.VMEM((rank, depth), f32),
            pltpu.VMEM((rank, cols), f32),
            pltpu.VMEM((tensors, toks // 2, 2 * rank), bf16),
            pltpu.VMEM((chips, toks, cols), f32),
            pltpu.VMEM((chips, toks, cols), bf16),
            pltpu.VMEM((chips, toks, cols), bf16),
            pltpu.VMEM((chips - 1, toks, cols), bf16),
            pltpu.VMEM((chips - 1, toks, cols), bf16),
            dma((4,)),
            dma((rows,)),
            dma((rows,)),
            dma((chips,)),
            pltpu.SemaphoreType.REGULAR((2,)),
            dma((2,)),
            dma((2,)),
            dma((2,)),
            dma,
            dma,
            dma((chips,)),
            dma((chips,)),
            dma((chips - 1,)),
            dma((chips - 1,)),
        ],
        compiler_params=pltpu.CompilerParams(
            collective_id=0, has_side_effects=True, vmem_limit_bytes=VMEM_BYTES
        ),
    )(
        queries,
        keys[:, 0],
        values[:, 0],
        step_keys[:, :, 0],
        step_values[:, :, 0],
        lengths[None, :],
        weight,
        down.T,
        up,
    )


def solution(mesh):
    return jax.shard_map(
        functools.partial(on_device, (mesh.shape["group"], mesh.shape["tensor"])),
        mesh=mesh,
        in_specs=(
            P(None, "group", "tensor"),
            P("group", "tensor", None, None),
            P("group", "tensor", None, None),
            P(None, "group", "tensor", None),
            P(None, "group", "tensor", None),
            P("group"),
            P("tensor", None),
            P("tensor", "group"),
            P("group", "tensor"),
        ),
        out_specs=P(None, "group", "tensor"),
        check_vma=False,
    )
```

```python
import functools
import math

import jax
import jax.numpy as jnp
from jax import lax
from jax.experimental import pallas as pl
from jax.experimental.pallas import tpu as pltpu
from jax.sharding import PartitionSpec as P

MESH = pl.DeviceIdType.MESH
HEAD_SIZE = 128
QH = 2
EXP2_SCALE = HEAD_SIZE**-0.5 / math.log(2.0)
NEG = -1e30
VMEM_BYTES = 63 * 1024 * 1024


def nt_dot(a, b):
    return lax.dot_general(a, b, (((1,), (1,)), ((), ())), preferred_element_type=jnp.float32)


def kernel(
    groups,
    tensors,
    q_hbm,
    k_hbm,
    v_hbm,
    sk_hbm,
    sv_hbm,
    len_hbm,
    w_hbm,
    down_hbm,
    up_hbm,
    out_ref,
    q_v,
    k_v,
    v_v,
    sk_v,
    sv_v,
    len_v,
    w_v,
    down_v,
    up_v,
    gdown,
    gup,
    down_f,
    up_f,
    lows,
    keep,
    send1,
    recv1,
    send2,
    recv2,
    small_sem,
    k_sem,
    v_sem,
    w_sem,
    met_sem,
    mine_sem,
    sent_sem,
    come_sem,
    low_sent,
    low_sem,
    s1_sem,
    r1_sem,
    s2_sem,
    r2_sem,
):
    steps, rows, _ = q_v.shape
    cache = k_v.shape[0]
    toks = steps * rows
    cols = out_ref.shape[2]
    chips = tensors // 2
    rank = down_f.shape[0]

    g = lax.axis_index("group")
    t = lax.axis_index("tensor")
    chip = t // 2
    core = t % 2
    planes = groups // 2
    z = lax.rem(g, planes)
    order = 2 * z + g // planes
    late = (2 * z) // planes

    smalls = [
        pltpu.make_async_copy(src, dst, small_sem.at[i])
        for i, (src, dst) in enumerate(
            [
                (q_hbm, q_v),
                (sk_hbm, sk_v),
                (sv_hbm, sv_v),
                (len_hbm, len_v),
            ]
        )
    ]
    k_copies = [
        pltpu.make_async_copy(k_hbm.at[r], k_v.at[:, pl.ds(r * HEAD_SIZE, HEAD_SIZE)], k_sem.at[r])
        for r in range(rows)
    ]
    v_copies = [
        pltpu.make_async_copy(v_hbm.at[part], v_v.at[part], v_sem.at[i])
        for i, part in enumerate((pl.ds(0, rows // 2), pl.ds(rows // 2, rows // 2)))
    ]
    pair = 2 * cols

    def chunk_at(k):
        return lax.rem(chip + k + 1, chips)

    depth = w_v.shape[0]
    w_copies = [
        pltpu.make_async_copy(w_hbm.at[part], w_v.at[part], w_sem.at[i])
        for i, part in enumerate(pl.ds(i * (depth // 4), depth // 4) for i in range(4))
    ]
    mine_copies = [
        pltpu.make_async_copy(down_hbm, down_v, mine_sem.at[0]),
        pltpu.make_async_copy(up_hbm, up_v, mine_sem.at[1]),
    ]
    for c in mine_copies:
        c.start()


    barrier = pltpu.get_barrier_semaphore()
    home = t - core
    partner = {"tensor": home + 1 - core}
    half = groups // 2
    first_mail = late
    plane = 2 * (chips - 1)

    @pl.when(core != first_mail)
    def _():
        pl.semaphore_signal(barrier, inc=1, device_id=partner, device_id_type=MESH)

    def group_at(k):
        return lax.rem(k, 2) * planes + k // 2

    def greet():
        def greet_group(i, carry):
            away = (i + 1) // 2 * (1 - 2 * lax.rem(i, 2))
            k = lax.rem(order + half + away + groups, groups)
            there = k // half
            mail = late + there - 2 * late * there
            pl.semaphore_signal(
                barrier,
                inc=1,
                device_id={"group": group_at(k), "tensor": home + mail},
                device_id_type=MESH,
            )
            return carry

        lax.fori_loop(0, groups - 1, greet_group, 0)
        for k in range(chips - 1):
            pl.semaphore_signal(
                barrier, inc=1, device_id={"tensor": chunk_at(k) * 2}, device_id_type=MESH
            )

    def meet(which, mail, count):
        @pl.when(core == mail)
        def _():
            pl.semaphore_wait(barrier, count)
            pl.semaphore_signal(met_sem.at[which], inc=1, device_id=partner, device_id_type=MESH)

        @pl.when(core != mail)
        def _():
            pl.semaphore_wait(met_sem.at[which], 1)

    def meet_first():
        meet(0, first_mail, 2 * half + 1 + (1 - late) * (plane - 2))

    def meet_second():
        meet(1, 1 - first_mail, 2 * half + late * (plane - 2))

    def send_to(first, which):
        src, dst = ((down_v, gdown), (up_v, gup))[which]

        def send(k, carry):
            pltpu.make_async_remote_copy(
                src_ref=src,
                dst_ref=dst.at[order],
                send_sem=sent_sem.at[which],
                recv_sem=come_sem.at[which, late],
                device_id={"group": group_at(k)},
                device_id_type=MESH,
            ).start()
            return carry

        lax.fori_loop(first, jnp.clip(order, first, first + half), send, 0)
        lax.fori_loop(jnp.clip(order + 1, first, first + half), first + half, send, 0)

    def wait_mine():
        for c in mine_copies:
            c.wait()

    hurry = 4 * z >= planes

    last = (late == 1) & (4 * z < 3 * planes)
    pl.when(jnp.logical_not(last))(greet)
    for c in smalls + k_copies:
        c.start()
    wait_mine()

    @pl.when(hurry)
    def _():
        meet_first()
        send_to(0, 0)

    pl.when(last)(greet)

    for c in v_copies + w_copies:
        c.start()

    for c in smalls:
        c.wait()
    q32 = jnp.concatenate([q_v[s].astype(jnp.float32) for s in range(steps)], axis=0)
    q64 = jnp.concatenate([q32[:, h * HEAD_SIZE : (h + 1) * HEAD_SIZE] for h in range(QH)], axis=0)
    height = QH * toks
    row_of = lax.broadcasted_iota(jnp.int32, (height, 1), 0) % rows
    step_of = (lax.broadcasted_iota(jnp.int32, (height, 1), 0) // rows) % steps
    q_wide = jnp.concatenate(
        [jnp.where(row_of == r, q64, 0.0).astype(jnp.bfloat16) for r in range(rows)], axis=1
    )
    sk = jnp.concatenate([sk_v[s].astype(jnp.float32) for s in range(steps)], axis=0)
    sv = jnp.concatenate([sv_v[s].astype(jnp.float32) for s in range(steps)], axis=0)
    recent = nt_dot(q64.astype(jnp.bfloat16), sk.astype(jnp.bfloat16))
    col = lax.broadcasted_iota(jnp.int32, (height, toks), 1)
    recent = jnp.where((col % rows == row_of) & (col // rows <= step_of), recent, NEG)
    lane = lax.broadcasted_iota(jnp.int32, (rows, rows), 1)
    sub = lax.broadcasted_iota(jnp.int32, (rows, rows), 0)
    lens = jnp.sum(
        jnp.where(lane == sub, jnp.broadcast_to(len_v[...], (rows, rows)), 0).astype(jnp.float32),
        axis=1,
        keepdims=True,
    )
    lens = jnp.concatenate([lens] * (QH * steps), axis=0)
    for c in k_copies:
        c.wait()
    cached = nt_dot(q_wide, k_v[...])
    position = lax.broadcasted_iota(jnp.int32, (height, cache), 1).astype(jnp.float32)
    cached = jnp.where(position < lens, cached, NEG)
    top = jnp.maximum(
        jnp.max(cached, axis=1, keepdims=True), jnp.max(recent, axis=1, keepdims=True)
    )
    cached = jnp.exp2((cached - top) * EXP2_SCALE)
    recent = jnp.exp2((recent - top) * EXP2_SCALE)
    norm = 1.0 / (
        jnp.sum(cached, axis=1, keepdims=True) + jnp.sum(recent, axis=1, keepdims=True)
    )
    cached = cached * norm
    recent = (recent * norm).astype(jnp.bfloat16)
    for c in v_copies:
        c.wait()
    mixed = jnp.dot(recent, sv.astype(jnp.bfloat16), preferred_element_type=jnp.float32)
    weights = jnp.concatenate(
        [jnp.where(row_of == r, cached, 0.0).astype(jnp.bfloat16) for r in range(rows)], axis=1
    )
    mixed = mixed + jnp.dot(
        weights, v_v[...].reshape(rows * cache, HEAD_SIZE), preferred_element_type=jnp.float32)
    attended = jnp.concatenate([mixed[h * toks : (h + 1) * toks] for h in range(QH)], axis=1)
    attended = attended.astype(jnp.bfloat16)

    pl.when(hurry)(lambda: send_to(0, 1))

    @pl.when(late == 1)
    def _():
        meet_second()
        send_to(half, 0)

    for c in w_copies:
        c.wait()
    for k in range(chips):
        part = jnp.dot(
            attended, w_v[:, k * pair : (k + 1) * pair], preferred_element_type=jnp.float32
        )
        first, second = part[:, :cols], part[:, cols:]
        keep[k, :, :] = jnp.where(core == 0, first, second)
        send1[k, :, :] = jnp.where(core == 0, second, first).astype(jnp.bfloat16)

    @pl.when(jnp.logical_not(hurry))
    def _():
        meet_first()
        send_to(0, 0)
        send_to(0, 1)


    to_partner = []
    for k in range(chips):
        copy = pltpu.make_async_remote_copy(
            src_ref=send1.at[chunk_at(k)],
            dst_ref=recv1.at[k],
            send_sem=s1_sem.at[k],
            recv_sem=r1_sem.at[k],
            device_id={"tensor": t + 1 - 2 * core},
            device_id_type=MESH,
        )
        copy.start()
        to_partner.append(copy)

    to_chips = []
    for k in range(chips):
        to_partner[k].wait_recv()
        both = keep[chunk_at(k)] + recv1[k].astype(jnp.float32)
        if k < chips - 1:
            send2[k, :, :] = both.astype(jnp.bfloat16)
            copy = pltpu.make_async_remote_copy(
                src_ref=send2.at[k],
                dst_ref=recv2.at[k],
                send_sem=s2_sem.at[k],
                recv_sem=r2_sem.at[k],
                device_id={"tensor": chunk_at(k) * 2 + core},
                device_id_type=MESH,
            )
            copy.start()
            to_chips.append(copy)
        else:
            total = both

    @pl.when(late == 0)
    def _():
        meet_second()
        send_to(half, 0)

    gdown[order] = down_v[...]
    gup[order] = up_v[...]
    downs = gdown.at[pl.ds(0, groups - 1)]
    ups = gup.at[pl.ds(0, groups - 1)]

    def wait_half(which, buffer, h):
        for mine in (0, 1):
            blocks = buffer.at[pl.ds(0, half - mine)]

            @pl.when((late == h) == (mine == 1))
            def _():
                pltpu.make_async_copy(blocks, blocks, come_sem.at[which, h]).wait()


    per = gdown.shape[1]
    for h in range(2):
        wait_half(0, gdown, h)
        for i in range(h * half, (h + 1) * half):
            down_f[per * i : per * (i + 1), :] = gdown[i].astype(jnp.float32)
    low = nt_dot(attended, down_f[...].astype(jnp.bfloat16))
    top_rows = toks // 2
    low = jnp.concatenate([low[:top_rows], low[top_rows:]], axis=1)
    lows[tensors - 1, :, :] = low.astype(jnp.bfloat16)
    xs = chips // 2
    steps_away = sorted(
        ((a, b, c) for a in range(2) for b in range(xs) for c in range(2) if a + b + c),
        key=lambda s: (-2 * s[0] - min(s[1], xs - s[1]), s[2]),
    )
    far_first = [
        lax.rem(t // (2 * xs) + a, 2) * 2 * xs
        + lax.rem(lax.rem(chip, xs) + b, xs) * 2
        + lax.rem(core + c, 2)
        for a, b, c in steps_away
    ]
    low_copies = [
        pltpu.make_async_remote_copy(
            src_ref=lows.at[tensors - 1],
            dst_ref=lows.at[d],
            send_sem=low_sent,
            recv_sem=low_sem,
            device_id={"tensor": other},
            device_id_type=MESH,
        )
        for d, other in enumerate(far_first)
    ]
    for copy in low_copies:
        copy.start()

    send_to(half, 1)
    for h in range(2):
        wait_half(1, gup, h)
    for i in range(groups):
        up_f[per * i : per * (i + 1), :] = gup[i].astype(jnp.float32)
    up = up_f[...].astype(jnp.bfloat16)
    up = jnp.concatenate([up, up], axis=0)
    for k in range(chips - 1):
        to_chips[k].wait_recv()
        total = total + recv2[k].astype(jnp.float32)
    others = lows.at[pl.ds(0, tensors - 1)]
    pltpu.make_async_copy(others, others, low_sem).wait()
    low = lows[0].astype(jnp.float32)
    for d in range(1, tensors):
        low = low + lows[d].astype(jnp.float32)
    left = lax.broadcasted_iota(jnp.int32, low.shape, 1) < rank
    low = jnp.concatenate([jnp.where(left, low, 0.0), jnp.where(left, 0.0, low)], axis=0)
    high = low.astype(jnp.bfloat16)
    rest = (low - high.astype(jnp.float32)).astype(jnp.bfloat16)
    delta = jnp.dot(high, up, preferred_element_type=jnp.float32) + jnp.dot(
        rest, up, preferred_element_type=jnp.float32
    )
    result = (total + 2.0 * delta).astype(out_ref.dtype)
    for s in range(steps):
        out_ref[s, :, :] = result[s * rows : (s + 1) * rows]

    pltpu.make_async_copy(others, others, low_sent).wait()
    pltpu.make_async_copy(downs, downs, sent_sem.at[0]).wait()
    pltpu.make_async_copy(ups, ups, sent_sem.at[1]).wait()
    for copy in to_partner + to_chips:
        copy.wait_send()


def on_device(mesh_shape, queries, keys, values, step_keys, step_values, lengths, weight, down, up):
    groups, tensors = mesh_shape
    steps, rows, width = queries.shape
    cache = keys.shape[2]
    depth, per = down.shape
    cols = up.shape[1]
    chips = tensors // 2
    toks = steps * rows
    rank = per * groups
    bf16, f32 = jnp.bfloat16, jnp.float32
    hbm = pl.BlockSpec(memory_space=pltpu.HBM)
    dma = pltpu.SemaphoreType.DMA
    return pl.pallas_call(
        functools.partial(kernel, groups, tensors),
        out_shape=pltpu.VMEM((steps, rows, cols), bf16),
        in_specs=[hbm] * 9,
        out_specs=pl.BlockSpec(memory_space=pltpu.VMEM),
        scratch_shapes=[
            pltpu.VMEM((steps, rows, width), bf16),
            pltpu.VMEM((cache, rows * HEAD_SIZE), bf16),
            pltpu.VMEM((rows, cache, HEAD_SIZE), bf16),
            pltpu.VMEM((steps, rows, HEAD_SIZE), bf16),
            pltpu.VMEM((steps, rows, HEAD_SIZE), bf16),
            pltpu.VMEM((1, rows), jnp.int32),
            pltpu.VMEM((depth, weight.shape[1]), bf16),
            pltpu.VMEM((per, depth), bf16),
            pltpu.VMEM((per, cols), bf16),
            pltpu.VMEM((groups, per, depth), bf16),
            pltpu.VMEM((groups, per, cols), bf16),
            pltpu.VMEM((rank, depth), f32),
            pltpu.VMEM((rank, cols), f32),
            pltpu.VMEM((tensors, toks // 2, 2 * rank), bf16),
            pltpu.VMEM((chips, toks, cols), f32),
            pltpu.VMEM((chips, toks, cols), bf16),
            pltpu.VMEM((chips, toks, cols), bf16),
            pltpu.VMEM((chips - 1, toks, cols), bf16),
            pltpu.VMEM((chips - 1, toks, cols), bf16),
            dma((4,)),
            dma((rows,)),
            dma((2,)),
            dma((4,)),
            pltpu.SemaphoreType.REGULAR((2,)),
            dma((2,)),
            dma((2,)),
            dma((2, 2)),
            dma,
            dma,
            dma((chips,)),
            dma((chips,)),
            dma((chips - 1,)),
            dma((chips - 1,)),
        ],
        compiler_params=pltpu.CompilerParams(
            collective_id=0, has_side_effects=True, vmem_limit_bytes=VMEM_BYTES
        ),
    )(
        queries,
        keys[:, 0],
        values[:, 0],
        step_keys[:, :, 0],
        step_values[:, :, 0],
        lengths[None, :],
        weight,
        down.T,
        up,
    )


def solution(mesh):
    return jax.shard_map(
        functools.partial(on_device, (mesh.shape["group"], mesh.shape["tensor"])),
        mesh=mesh,
        in_specs=(
            P(None, "group", "tensor"),
            P("group", "tensor", None, None),
            P("group", "tensor", None, None),
            P(None, "group", "tensor", None),
            P(None, "group", "tensor", None),
            P("group"),
            P("tensor", None),
            P("tensor", "group"),
            P("group", "tensor"),
        ),
        out_specs=P(None, "group", "tensor"),
        check_vma=False,
    )
```

```python
import functools
import math

import jax
import jax.numpy as jnp
from jax import lax
from jax.experimental import pallas as pl
from jax.experimental.pallas import tpu as pltpu
from jax.sharding import PartitionSpec as P

MESH = pl.DeviceIdType.MESH
HEAD_SIZE = 128
QH = 2
EXP2_SCALE = HEAD_SIZE**-0.5 / math.log(2.0)
NEG = -1e30
VMEM_BYTES = 63 * 1024 * 1024


def nt_dot(a, b):
    return lax.dot_general(a, b, (((1,), (1,)), ((), ())), preferred_element_type=jnp.float32)


def kernel(
    groups,
    tensors,
    q_hbm,
    k_hbm,
    v_hbm,
    sk_hbm,
    sv_hbm,
    len_hbm,
    w_hbm,
    down_hbm,
    up_hbm,
    out_ref,
    q_v,
    k_v,
    v_v,
    sk_v,
    sv_v,
    len_v,
    w_v,
    down_v,
    up_v,
    gdown,
    gup,
    down_f,
    up_f,
    lows,
    keep,
    send1,
    recv1,
    send2,
    recv2,
    small_sem,
    k_sem,
    v_sem,
    w_sem,
    met_sem,
    mine_sem,
    sent_sem,
    come_sem,
    low_sent,
    low_sem,
    s1_sem,
    r1_sem,
    s2_sem,
    r2_sem,
):
    steps, rows, _ = q_v.shape
    cache = k_v.shape[0]
    toks = steps * rows
    cols = out_ref.shape[2]
    chips = tensors // 2
    rank = down_f.shape[0]

    g = lax.axis_index("group")
    t = lax.axis_index("tensor")
    chip = t // 2
    core = t % 2
    planes = groups // 2
    z = lax.rem(g, planes)
    order = 2 * z + g // planes
    late = (2 * z) // planes

    smalls = [
        pltpu.make_async_copy(src, dst, small_sem.at[i])
        for i, (src, dst) in enumerate(
            [
                (q_hbm, q_v),
                (sk_hbm, sk_v),
                (sv_hbm, sv_v),
                (len_hbm, len_v),
            ]
        )
    ]
    k_copies = [
        pltpu.make_async_copy(k_hbm.at[r], k_v.at[:, pl.ds(r * HEAD_SIZE, HEAD_SIZE)], k_sem.at[r])
        for r in range(rows)
    ]
    v_copies = [
        pltpu.make_async_copy(v_hbm.at[part], v_v.at[part], v_sem.at[i])
        for i, part in enumerate((pl.ds(0, rows // 2), pl.ds(rows // 2, rows // 2)))
    ]
    pair = 2 * cols

    def chunk_at(k):
        return lax.rem(chip + k + 1, chips)

    depth = w_v.shape[0]
    w_copies = [
        pltpu.make_async_copy(w_hbm.at[part], w_v.at[part], w_sem.at[i])
        for i, part in enumerate(pl.ds(i * (depth // 4), depth // 4) for i in range(4))
    ]
    mine_copies = [
        pltpu.make_async_copy(down_hbm, down_v, mine_sem.at[0]),
        pltpu.make_async_copy(up_hbm, up_v, mine_sem.at[1]),
    ]
    for c in mine_copies:
        c.start()


    barrier = pltpu.get_barrier_semaphore()
    home = t - core
    partner = {"tensor": home + 1 - core}
    half = groups // 2
    first_mail = late
    hurry = 4 * z >= planes
    calm = jnp.where(hurry, 0, 1)
    quarter = groups // 4
    plane = 2 * (chips - 1)

    @pl.when(core != first_mail)
    def _():
        pl.semaphore_signal(barrier, inc=1, device_id=partner, device_id_type=MESH)

    def group_at(k):
        return lax.rem(k, 2) * planes + k // 2

    def greet():
        def greet_group(i, carry):
            away = (i + 1) // 2 * (1 - 2 * lax.rem(i, 2))
            k = lax.rem(order + half + away + groups, groups)
            there = k // half
            mail = late + there - 2 * late * there
            mail = jnp.where(k < quarter, 1 - calm, mail)
            pl.semaphore_signal(
                barrier,
                inc=1,
                device_id={"group": group_at(k), "tensor": home + mail},
                device_id_type=MESH,
            )
            return carry

        lax.fori_loop(0, groups - 1, greet_group, 0)
        for k in range(chips - 1):
            pl.semaphore_signal(
                barrier,
                inc=1,
                device_id={"tensor": chunk_at(k) * 2 + (1 - late) * (1 - calm)},
                device_id_type=MESH,
            )

    def meet(which, mail, count):
        @pl.when(core == mail)
        def _():
            pl.semaphore_wait(barrier, count)
            pl.semaphore_signal(met_sem.at[which], inc=1, device_id=partner, device_id_type=MESH)

        @pl.when(core != mail)
        def _():
            pl.semaphore_wait(met_sem.at[which], 1)

    def meet_first():
        others = jnp.where(hurry, half - 1 + late, quarter - 1)
        meet(0, first_mail, 2 * others + 1 + calm * plane)

    def meet_second():
        others = jnp.where(hurry, half - late, groups - quarter)
        meet(1, 1 - first_mail, 2 * others + (1 - calm) * plane)

    def send_to(first, last, which):
        src, dst = ((down_v, gdown), (up_v, gup))[which]

        def send(k, carry):
            pltpu.make_async_remote_copy(
                src_ref=src,
                dst_ref=dst.at[order],
                send_sem=sent_sem.at[which],
                recv_sem=come_sem.at[which, late],
                device_id={"group": group_at(k)},
                device_id_type=MESH,
            ).start()
            return carry

        lax.fori_loop(first, jnp.clip(order, first, last), send, 0)
        lax.fori_loop(jnp.clip(order + 1, first, last), last, send, 0)

    def wait_mine():
        for c in mine_copies:
            c.wait()


    last = (late == 1) & (4 * z < 3 * planes)
    pl.when(jnp.logical_not(last))(greet)
    for c in smalls + k_copies:
        c.start()
    wait_mine()

    @pl.when(hurry)
    def _():
        meet_first()
        send_to(0, half, 0)

    pl.when(last)(greet)

    for c in v_copies + w_copies:
        c.start()

    for c in smalls:
        c.wait()
    q32 = jnp.concatenate([q_v[s].astype(jnp.float32) for s in range(steps)], axis=0)
    q64 = jnp.concatenate([q32[:, h * HEAD_SIZE : (h + 1) * HEAD_SIZE] for h in range(QH)], axis=0)
    height = QH * toks
    row_of = lax.broadcasted_iota(jnp.int32, (height, 1), 0) % rows
    step_of = (lax.broadcasted_iota(jnp.int32, (height, 1), 0) // rows) % steps
    q_wide = jnp.concatenate(
        [jnp.where(row_of == r, q64, 0.0).astype(jnp.bfloat16) for r in range(rows)], axis=1
    )
    sk = jnp.concatenate([sk_v[s].astype(jnp.float32) for s in range(steps)], axis=0)
    sv = jnp.concatenate([sv_v[s].astype(jnp.float32) for s in range(steps)], axis=0)
    recent = nt_dot(q64.astype(jnp.bfloat16), sk.astype(jnp.bfloat16))
    col = lax.broadcasted_iota(jnp.int32, (height, toks), 1)
    recent = jnp.where((col % rows == row_of) & (col // rows <= step_of), recent, NEG)
    lane = lax.broadcasted_iota(jnp.int32, (rows, rows), 1)
    sub = lax.broadcasted_iota(jnp.int32, (rows, rows), 0)
    lens = jnp.sum(
        jnp.where(lane == sub, jnp.broadcast_to(len_v[...], (rows, rows)), 0).astype(jnp.float32),
        axis=1,
        keepdims=True,
    )
    lens = jnp.concatenate([lens] * (QH * steps), axis=0)
    for c in k_copies:
        c.wait()
    cached = nt_dot(q_wide, k_v[...])
    position = lax.broadcasted_iota(jnp.int32, (height, cache), 1).astype(jnp.float32)
    cached = jnp.where(position < lens, cached, NEG)
    top = jnp.maximum(
        jnp.max(cached, axis=1, keepdims=True), jnp.max(recent, axis=1, keepdims=True)
    )
    cached = jnp.exp2((cached - top) * EXP2_SCALE)
    recent = jnp.exp2((recent - top) * EXP2_SCALE)
    norm = 1.0 / (
        jnp.sum(cached, axis=1, keepdims=True) + jnp.sum(recent, axis=1, keepdims=True)
    )
    cached = cached * norm
    recent = (recent * norm).astype(jnp.bfloat16)
    for c in v_copies:
        c.wait()
    mixed = jnp.dot(recent, sv.astype(jnp.bfloat16), preferred_element_type=jnp.float32)
    weights = jnp.concatenate(
        [jnp.where(row_of == r, cached, 0.0).astype(jnp.bfloat16) for r in range(rows)], axis=1
    )
    mixed = mixed + jnp.dot(
        weights, v_v[...].reshape(rows * cache, HEAD_SIZE), preferred_element_type=jnp.float32)
    attended = jnp.concatenate([mixed[h * toks : (h + 1) * toks] for h in range(QH)], axis=1)
    attended = attended.astype(jnp.bfloat16)

    pl.when(hurry)(lambda: send_to(0, half, 1))

    @pl.when(late == 1)
    def _():
        meet_second()
        send_to(half, groups, 0)

    for c in w_copies:
        c.wait()
    for k in range(chips):
        part = jnp.dot(
            attended, w_v[:, k * pair : (k + 1) * pair], preferred_element_type=jnp.float32
        )
        first, second = part[:, :cols], part[:, cols:]
        keep[k, :, :] = jnp.where(core == 0, first, second)
        send1[k, :, :] = jnp.where(core == 0, second, first).astype(jnp.bfloat16)

    @pl.when(hurry & (late == 0))
    def _():
        meet_second()
        send_to(half, groups, 0)

    @pl.when(jnp.logical_not(hurry))
    def _():
        meet_first()
        send_to(0, quarter, 0)
        send_to(0, quarter, 1)


    to_partner = []
    for k in range(chips):
        copy = pltpu.make_async_remote_copy(
            src_ref=send1.at[chunk_at(k)],
            dst_ref=recv1.at[k],
            send_sem=s1_sem.at[k],
            recv_sem=r1_sem.at[k],
            device_id={"tensor": t + 1 - 2 * core},
            device_id_type=MESH,
        )
        copy.start()
        to_partner.append(copy)

    to_chips = []
    for k in range(chips):
        to_partner[k].wait_recv()
        both = keep[chunk_at(k)] + recv1[k].astype(jnp.float32)
        if k < chips - 1:
            send2[k, :, :] = both.astype(jnp.bfloat16)
            copy = pltpu.make_async_remote_copy(
                src_ref=send2.at[k],
                dst_ref=recv2.at[k],
                send_sem=s2_sem.at[k],
                recv_sem=r2_sem.at[k],
                device_id={"tensor": chunk_at(k) * 2 + core},
                device_id_type=MESH,
            )
            copy.start()
            to_chips.append(copy)
        else:
            total = both

    @pl.when(jnp.logical_not(hurry))
    def _():
        meet_second()
        send_to(quarter, groups, 0)

    gdown[order] = down_v[...]
    gup[order] = up_v[...]
    downs = gdown.at[pl.ds(0, groups - 1)]
    ups = gup.at[pl.ds(0, groups - 1)]

    def wait_half(which, buffer, h):
        for mine in (0, 1):
            blocks = buffer.at[pl.ds(0, half - mine)]

            @pl.when((late == h) == (mine == 1))
            def _():
                pltpu.make_async_copy(blocks, blocks, come_sem.at[which, h]).wait()


    per = gdown.shape[1]
    for h in range(2):
        wait_half(0, gdown, h)
        for i in range(h * half, (h + 1) * half):
            down_f[per * i : per * (i + 1), :] = gdown[i].astype(jnp.float32)
    low = nt_dot(attended, down_f[...].astype(jnp.bfloat16))
    top_rows = toks // 2
    low = jnp.concatenate([low[:top_rows], low[top_rows:]], axis=1)
    lows[tensors - 1, :, :] = low.astype(jnp.bfloat16)
    xs = chips // 2
    steps_away = sorted(
        ((a, b, c) for a in range(2) for b in range(xs) for c in range(2) if a + b + c),
        key=lambda s: (-2 * s[0] - min(s[1], xs - s[1]), s[2]),
    )
    far_first = [
        lax.rem(t // (2 * xs) + a, 2) * 2 * xs
        + lax.rem(lax.rem(chip, xs) + b, xs) * 2
        + lax.rem(core + c, 2)
        for a, b, c in steps_away
    ]
    low_copies = [
        pltpu.make_async_remote_copy(
            src_ref=lows.at[tensors - 1],
            dst_ref=lows.at[d],
            send_sem=low_sent,
            recv_sem=low_sem,
            device_id={"tensor": other},
            device_id_type=MESH,
        )
        for d, other in enumerate(far_first)
    ]
    for copy in low_copies:
        copy.start()

    pl.when(hurry)(lambda: send_to(half, groups, 1))
    pl.when(jnp.logical_not(hurry))(lambda: send_to(quarter, groups, 1))
    for h in range(2):
        wait_half(1, gup, h)
    for i in range(groups):
        up_f[per * i : per * (i + 1), :] = gup[i].astype(jnp.float32)
    up = up_f[...].astype(jnp.bfloat16)
    up = jnp.concatenate([up, up], axis=0)
    for k in range(chips - 1):
        to_chips[k].wait_recv()
        total = total + recv2[k].astype(jnp.float32)
    others = lows.at[pl.ds(0, tensors - 1)]
    pltpu.make_async_copy(others, others, low_sent).wait()
    pltpu.make_async_copy(downs, downs, sent_sem.at[0]).wait()
    pltpu.make_async_copy(ups, ups, sent_sem.at[1]).wait()
    for copy in to_partner + to_chips:
        copy.wait_send()

    pltpu.make_async_copy(others, others, low_sem).wait()
    low = lows[0].astype(jnp.float32)
    for d in range(1, tensors):
        low = low + lows[d].astype(jnp.float32)
    left = lax.broadcasted_iota(jnp.int32, low.shape, 1) < rank
    low = jnp.concatenate([jnp.where(left, low, 0.0), jnp.where(left, 0.0, low)], axis=0)
    high = low.astype(jnp.bfloat16)
    rest = (low - high.astype(jnp.float32)).astype(jnp.bfloat16)
    delta = jnp.dot(
        jnp.concatenate([high, rest], axis=0), up, preferred_element_type=jnp.float32
    )
    delta = delta[:toks] + delta[toks:]
    result = (total + 2.0 * delta).astype(out_ref.dtype)
    for s in range(steps):
        out_ref[s, :, :] = result[s * rows : (s + 1) * rows]

def on_device(mesh_shape, queries, keys, values, step_keys, step_values, lengths, weight, down, up):
    groups, tensors = mesh_shape
    steps, rows, width = queries.shape
    cache = keys.shape[2]
    depth, per = down.shape
    cols = up.shape[1]
    chips = tensors // 2
    toks = steps * rows
    rank = per * groups
    bf16, f32 = jnp.bfloat16, jnp.float32
    hbm = pl.BlockSpec(memory_space=pltpu.HBM)
    dma = pltpu.SemaphoreType.DMA
    return pl.pallas_call(
        functools.partial(kernel, groups, tensors),
        out_shape=pltpu.VMEM((steps, rows, cols), bf16),
        in_specs=[hbm] * 9,
        out_specs=pl.BlockSpec(memory_space=pltpu.VMEM),
        scratch_shapes=[
            pltpu.VMEM((steps, rows, width), bf16),
            pltpu.VMEM((cache, rows * HEAD_SIZE), bf16),
            pltpu.VMEM((rows, cache, HEAD_SIZE), bf16),
            pltpu.VMEM((steps, rows, HEAD_SIZE), bf16),
            pltpu.VMEM((steps, rows, HEAD_SIZE), bf16),
            pltpu.VMEM((1, rows), jnp.int32),
            pltpu.VMEM((depth, weight.shape[1]), bf16),
            pltpu.VMEM((per, depth), bf16),
            pltpu.VMEM((per, cols), bf16),
            pltpu.VMEM((groups, per, depth), bf16),
            pltpu.VMEM((groups, per, cols), bf16),
            pltpu.VMEM((rank, depth), f32),
            pltpu.VMEM((rank, cols), f32),
            pltpu.VMEM((tensors, toks // 2, 2 * rank), bf16),
            pltpu.VMEM((chips, toks, cols), f32),
            pltpu.VMEM((chips, toks, cols), bf16),
            pltpu.VMEM((chips, toks, cols), bf16),
            pltpu.VMEM((chips - 1, toks, cols), bf16),
            pltpu.VMEM((chips - 1, toks, cols), bf16),
            dma((4,)),
            dma((rows,)),
            dma((2,)),
            dma((4,)),
            pltpu.SemaphoreType.REGULAR((2,)),
            dma((2,)),
            dma((2,)),
            dma((2, 2)),
            dma,
            dma,
            dma((chips,)),
            dma((chips,)),
            dma((chips - 1,)),
            dma((chips - 1,)),
        ],
        compiler_params=pltpu.CompilerParams(
            collective_id=0, has_side_effects=True, vmem_limit_bytes=VMEM_BYTES
        ),
    )(
        queries,
        keys[:, 0],
        values[:, 0],
        step_keys[:, :, 0],
        step_values[:, :, 0],
        lengths[None, :],
        weight,
        down.T,
        up,
    )


def solution(mesh):
    return jax.shard_map(
        functools.partial(on_device, (mesh.shape["group"], mesh.shape["tensor"])),
        mesh=mesh,
        in_specs=(
            P(None, "group", "tensor"),
            P("group", "tensor", None, None),
            P("group", "tensor", None, None),
            P(None, "group", "tensor", None),
            P(None, "group", "tensor", None),
            P("group"),
            P("tensor", None),
            P("tensor", "group"),
            P("group", "tensor"),
        ),
        out_specs=P(None, "group", "tensor"),
        check_vma=False,
    )
```

```python
import functools
import math

import jax
import jax.numpy as jnp
from jax import lax
from jax.experimental import pallas as pl
from jax.experimental.pallas import tpu as pltpu
from jax.sharding import PartitionSpec as P

MESH = pl.DeviceIdType.MESH
HEAD_SIZE = 128
QH = 2
EXP2_SCALE = HEAD_SIZE**-0.5 / math.log(2.0)
NEG = -1e30
VMEM_BYTES = 63 * 1024 * 1024


def nt_dot(a, b):
    return lax.dot_general(a, b, (((1,), (1,)), ((), ())), preferred_element_type=jnp.float32)


def kernel(
    groups,
    tensors,
    q_hbm,
    k_hbm,
    v_hbm,
    sk_hbm,
    sv_hbm,
    len_hbm,
    w_hbm,
    down_hbm,
    up_hbm,
    out_ref,
    q_v,
    k_v,
    v_v,
    sk_v,
    sv_v,
    len_v,
    w_v,
    down_v,
    up_v,
    gdown,
    gup,
    down_f,
    up_f,
    lows,
    keep,
    send1,
    recv1,
    send2,
    recv2,
    small_sem,
    k_sem,
    v_sem,
    w_sem,
    met_sem,
    mine_sem,
    sent_sem,
    come_sem,
    low_sent,
    low_sem,
    s1_sem,
    r1_sem,
    s2_sem,
    r2_sem,
):
    steps, rows, _ = q_v.shape
    cache = k_v.shape[0]
    toks = steps * rows
    cols = out_ref.shape[2]
    chips = tensors // 2
    rank = down_f.shape[0]

    g = lax.axis_index("group")
    t = lax.axis_index("tensor")
    chip = t // 2
    core = t % 2
    planes = groups // 2
    z = lax.rem(g, planes)
    order = 2 * z + g // planes
    late = (2 * z) // planes

    smalls = [
        pltpu.make_async_copy(src, dst, small_sem.at[i])
        for i, (src, dst) in enumerate(
            [
                (q_hbm, q_v),
                (sk_hbm, sk_v),
                (sv_hbm, sv_v),
                (len_hbm, len_v),
            ]
        )
    ]
    k_copies = [
        pltpu.make_async_copy(k_hbm.at[r], k_v.at[:, pl.ds(r * HEAD_SIZE, HEAD_SIZE)], k_sem.at[r])
        for r in range(rows)
    ]
    v_copies = [
        pltpu.make_async_copy(v_hbm.at[part], v_v.at[part], v_sem.at[i])
        for i, part in enumerate((pl.ds(0, rows // 2), pl.ds(rows // 2, rows // 2)))
    ]
    pair = 2 * cols

    def chunk_at(k):
        return lax.rem(chip + k + 1, chips)

    depth = w_v.shape[0]
    w_copies = [
        pltpu.make_async_copy(w_hbm.at[part], w_v.at[part], w_sem.at[i])
        for i, part in enumerate(pl.ds(i * (depth // 4), depth // 4) for i in range(4))
    ]
    mine_copies = [
        pltpu.make_async_copy(down_hbm, down_v, mine_sem.at[0]),
        pltpu.make_async_copy(up_hbm, up_v, mine_sem.at[1]),
    ]
    for c in mine_copies:
        c.start()


    barrier = pltpu.get_barrier_semaphore()
    home = t - core
    partner = {"tensor": home + 1 - core}
    half = groups // 2
    first_mail = late
    hurry = 4 * z >= planes
    calm = jnp.where(hurry, 0, 1)
    quarter = groups // 4
    plane = 2 * (chips - 1)

    @pl.when(core != first_mail)
    def _():
        pl.semaphore_signal(barrier, inc=1, device_id=partner, device_id_type=MESH)

    def group_at(k):
        return lax.rem(k, 2) * planes + k // 2

    def greet():
        def greet_group(i, carry):
            away = (i + 1) // 2 * (1 - 2 * lax.rem(i, 2))
            k = lax.rem(order + half + away + groups, groups)
            there = k // half
            mail = late + there - 2 * late * there
            mail = jnp.where(k < quarter, 1 - calm, mail)
            pl.semaphore_signal(
                barrier,
                inc=1,
                device_id={"group": group_at(k), "tensor": home + mail},
                device_id_type=MESH,
            )
            return carry

        lax.fori_loop(0, groups - 1, greet_group, 0)
        for k in range(chips - 1):
            pl.semaphore_signal(
                barrier,
                inc=1,
                device_id={"tensor": chunk_at(k) * 2 + (1 - late) * (1 - calm)},
                device_id_type=MESH,
            )

    def meet(which, mail, count):
        @pl.when(core == mail)
        def _():
            pl.semaphore_wait(barrier, count)
            pl.semaphore_signal(met_sem.at[which], inc=1, device_id=partner, device_id_type=MESH)

        @pl.when(core != mail)
        def _():
            pl.semaphore_wait(met_sem.at[which], 1)

    def meet_first():
        others = jnp.where(hurry, half - 1 + late, quarter - 1)
        meet(0, first_mail, 2 * others + 1 + calm * plane)

    def meet_second():
        others = jnp.where(hurry, half - late, groups - quarter)
        meet(1, 1 - first_mail, 2 * others + (1 - calm) * plane)

    def send_to(first, last, which):
        src, dst = ((down_v, gdown), (up_v, gup))[which]

        def send(k, carry):
            pltpu.make_async_remote_copy(
                src_ref=src,
                dst_ref=dst.at[order],
                send_sem=sent_sem.at[which],
                recv_sem=come_sem.at[which, late],
                device_id={"group": group_at(k)},
                device_id_type=MESH,
            ).start()
            return carry

        lax.fori_loop(first, jnp.clip(order, first, last), send, 0)
        lax.fori_loop(jnp.clip(order + 1, first, last), last, send, 0)

    def wait_mine():
        for c in mine_copies:
            c.wait()


    last = (late == 1) & (4 * z < 3 * planes)
    pl.when(jnp.logical_not(last))(greet)
    for c in smalls + k_copies:
        c.start(priority=1)
    wait_mine()

    @pl.when(hurry)
    def _():
        meet_first()
        send_to(0, half, 0)

    pl.when(last)(greet)

    for c in v_copies + w_copies:
        c.start(priority=1)

    for c in smalls:
        c.wait()
    q32 = jnp.concatenate([q_v[s].astype(jnp.float32) for s in range(steps)], axis=0)
    q64 = jnp.concatenate([q32[:, h * HEAD_SIZE : (h + 1) * HEAD_SIZE] for h in range(QH)], axis=0)
    height = QH * toks
    row_of = lax.broadcasted_iota(jnp.int32, (height, 1), 0) % rows
    step_of = (lax.broadcasted_iota(jnp.int32, (height, 1), 0) // rows) % steps
    q_wide = jnp.concatenate(
        [jnp.where(row_of == r, q64, 0.0).astype(jnp.bfloat16) for r in range(rows)], axis=1
    )
    sk = jnp.concatenate([sk_v[s].astype(jnp.float32) for s in range(steps)], axis=0)
    sv = jnp.concatenate([sv_v[s].astype(jnp.float32) for s in range(steps)], axis=0)
    recent = nt_dot(q64.astype(jnp.bfloat16), sk.astype(jnp.bfloat16))
    col = lax.broadcasted_iota(jnp.int32, (height, toks), 1)
    recent = jnp.where((col % rows == row_of) & (col // rows <= step_of), recent, NEG)
    lane = lax.broadcasted_iota(jnp.int32, (rows, rows), 1)
    sub = lax.broadcasted_iota(jnp.int32, (rows, rows), 0)
    lens = jnp.sum(
        jnp.where(lane == sub, jnp.broadcast_to(len_v[...], (rows, rows)), 0).astype(jnp.float32),
        axis=1,
        keepdims=True,
    )
    lens = jnp.concatenate([lens] * (QH * steps), axis=0)
    for c in k_copies:
        c.wait()
    cached = nt_dot(q_wide, k_v[...])
    position = lax.broadcasted_iota(jnp.int32, (height, cache), 1).astype(jnp.float32)
    cached = jnp.where(position < lens, cached, NEG)
    top = jnp.maximum(
        jnp.max(cached, axis=1, keepdims=True), jnp.max(recent, axis=1, keepdims=True)
    )
    cached = jnp.exp2((cached - top) * EXP2_SCALE)
    recent = jnp.exp2((recent - top) * EXP2_SCALE)
    norm = 1.0 / (
        jnp.sum(cached, axis=1, keepdims=True) + jnp.sum(recent, axis=1, keepdims=True)
    )
    cached = cached * norm
    recent = (recent * norm).astype(jnp.bfloat16)
    for c in v_copies:
        c.wait()
    mixed = jnp.dot(recent, sv.astype(jnp.bfloat16), preferred_element_type=jnp.float32)
    weights = jnp.concatenate(
        [jnp.where(row_of == r, cached, 0.0).astype(jnp.bfloat16) for r in range(rows)], axis=1
    )
    mixed = mixed + jnp.dot(
        weights, v_v[...].reshape(rows * cache, HEAD_SIZE), preferred_element_type=jnp.float32)
    attended = jnp.concatenate([mixed[h * toks : (h + 1) * toks] for h in range(QH)], axis=1)
    attended = attended.astype(jnp.bfloat16)

    pl.when(hurry)(lambda: send_to(0, half, 1))

    @pl.when(late == 1)
    def _():
        meet_second()
        send_to(half, groups, 0)

    for c in w_copies:
        c.wait()
    for k in range(chips):
        part = jnp.dot(
            attended, w_v[:, k * pair : (k + 1) * pair], preferred_element_type=jnp.float32
        )
        first, second = part[:, :cols], part[:, cols:]
        keep[k, :, :] = jnp.where(core == 0, first, second)
        send1[k, :, :] = jnp.where(core == 0, second, first).astype(jnp.bfloat16)

    @pl.when(hurry & (late == 0))
    def _():
        meet_second()
        send_to(half, groups, 0)

    @pl.when(jnp.logical_not(hurry))
    def _():
        meet_first()
        send_to(0, quarter, 0)
        send_to(0, quarter, 1)


    to_partner = []
    for k in range(chips):
        copy = pltpu.make_async_remote_copy(
            src_ref=send1.at[chunk_at(k)],
            dst_ref=recv1.at[k],
            send_sem=s1_sem.at[k],
            recv_sem=r1_sem.at[k],
            device_id={"tensor": t + 1 - 2 * core},
            device_id_type=MESH,
        )
        copy.start()
        to_partner.append(copy)

    to_chips = []
    for k in range(chips):
        to_partner[k].wait_recv()
        both = keep[chunk_at(k)] + recv1[k].astype(jnp.float32)
        if k < chips - 1:
            send2[k, :, :] = both.astype(jnp.bfloat16)
            copy = pltpu.make_async_remote_copy(
                src_ref=send2.at[k],
                dst_ref=recv2.at[k],
                send_sem=s2_sem.at[k],
                recv_sem=r2_sem.at[k],
                device_id={"tensor": chunk_at(k) * 2 + core},
                device_id_type=MESH,
            )
            copy.start()
            to_chips.append(copy)
        else:
            total = both

    @pl.when(jnp.logical_not(hurry))
    def _():
        meet_second()
        send_to(quarter, groups, 0)

    gdown[order] = down_v[...]
    gup[order] = up_v[...]
    downs = gdown.at[pl.ds(0, groups - 1)]
    ups = gup.at[pl.ds(0, groups - 1)]

    def wait_half(which, buffer, h):
        for mine in (0, 1):
            blocks = buffer.at[pl.ds(0, half - mine)]

            @pl.when((late == h) == (mine == 1))
            def _():
                pltpu.make_async_copy(blocks, blocks, come_sem.at[which, h]).wait()


    per = gdown.shape[1]
    for h in range(2):
        wait_half(0, gdown, h)
        for i in range(h * half, (h + 1) * half):
            down_f[per * i : per * (i + 1), :] = gdown[i].astype(jnp.float32)
    low = nt_dot(attended, down_f[...].astype(jnp.bfloat16))
    top_rows = toks // 2
    low = jnp.concatenate([low[:top_rows], low[top_rows:]], axis=1)
    lows[tensors - 1, :, :] = low.astype(jnp.bfloat16)
    xs = chips // 2
    steps_away = sorted(
        ((a, b, c) for a in range(2) for b in range(xs) for c in range(2) if a + b + c),
        key=lambda s: (-2 * s[0] - min(s[1], xs - s[1]), s[2]),
    )
    far_first = [
        lax.rem(t // (2 * xs) + a, 2) * 2 * xs
        + lax.rem(lax.rem(chip, xs) + b, xs) * 2
        + lax.rem(core + c, 2)
        for a, b, c in steps_away
    ]
    low_copies = [
        pltpu.make_async_remote_copy(
            src_ref=lows.at[tensors - 1],
            dst_ref=lows.at[d],
            send_sem=low_sent,
            recv_sem=low_sem,
            device_id={"tensor": other},
            device_id_type=MESH,
        )
        for d, other in enumerate(far_first)
    ]
    for copy in low_copies:
        copy.start()

    pl.when(hurry)(lambda: send_to(half, groups, 1))
    pl.when(jnp.logical_not(hurry))(lambda: send_to(quarter, groups, 1))
    for h in range(2):
        wait_half(1, gup, h)
    for i in range(groups):
        up_f[per * i : per * (i + 1), :] = gup[i].astype(jnp.float32)
    up = up_f[...].astype(jnp.bfloat16)
    up = jnp.concatenate([up, up], axis=0)
    for k in range(chips - 1):
        to_chips[k].wait_recv()
        total = total + recv2[k].astype(jnp.float32)
    others = lows.at[pl.ds(0, tensors - 1)]
    pltpu.make_async_copy(others, others, low_sent).wait()
    pltpu.make_async_copy(downs, downs, sent_sem.at[0]).wait()
    pltpu.make_async_copy(ups, ups, sent_sem.at[1]).wait()
    for copy in to_partner + to_chips:
        copy.wait_send()

    pltpu.make_async_copy(others, others, low_sem).wait()
    low = lows[0].astype(jnp.float32)
    for d in range(1, tensors):
        low = low + lows[d].astype(jnp.float32)
    left = lax.broadcasted_iota(jnp.int32, low.shape, 1) < rank
    low = jnp.concatenate([jnp.where(left, low, 0.0), jnp.where(left, 0.0, low)], axis=0)
    high = low.astype(jnp.bfloat16)
    rest = (low - high.astype(jnp.float32)).astype(jnp.bfloat16)
    delta = jnp.dot(
        jnp.concatenate([high, rest], axis=0), up, preferred_element_type=jnp.float32
    )
    delta = delta[:toks] + delta[toks:]
    result = (total + 2.0 * delta).astype(out_ref.dtype)
    for s in range(steps):
        out_ref[s, :, :] = result[s * rows : (s + 1) * rows]

def on_device(mesh_shape, queries, keys, values, step_keys, step_values, lengths, weight, down, up):
    groups, tensors = mesh_shape
    steps, rows, width = queries.shape
    cache = keys.shape[2]
    depth, per = down.shape
    cols = up.shape[1]
    chips = tensors // 2
    toks = steps * rows
    rank = per * groups
    bf16, f32 = jnp.bfloat16, jnp.float32
    hbm = pl.BlockSpec(memory_space=pltpu.HBM)
    dma = pltpu.SemaphoreType.DMA
    return pl.pallas_call(
        functools.partial(kernel, groups, tensors),
        out_shape=pltpu.VMEM((steps, rows, cols), bf16),
        in_specs=[hbm] * 9,
        out_specs=pl.BlockSpec(memory_space=pltpu.VMEM),
        scratch_shapes=[
            pltpu.VMEM((steps, rows, width), bf16),
            pltpu.VMEM((cache, rows * HEAD_SIZE), bf16),
            pltpu.VMEM((rows, cache, HEAD_SIZE), bf16),
            pltpu.VMEM((steps, rows, HEAD_SIZE), bf16),
            pltpu.VMEM((steps, rows, HEAD_SIZE), bf16),
            pltpu.VMEM((1, rows), jnp.int32),
            pltpu.VMEM((depth, weight.shape[1]), bf16),
            pltpu.VMEM((per, depth), bf16),
            pltpu.VMEM((per, cols), bf16),
            pltpu.VMEM((groups, per, depth), bf16),
            pltpu.VMEM((groups, per, cols), bf16),
            pltpu.VMEM((rank, depth), f32),
            pltpu.VMEM((rank, cols), f32),
            pltpu.VMEM((tensors, toks // 2, 2 * rank), bf16),
            pltpu.VMEM((chips, toks, cols), f32),
            pltpu.VMEM((chips, toks, cols), bf16),
            pltpu.VMEM((chips, toks, cols), bf16),
            pltpu.VMEM((chips - 1, toks, cols), bf16),
            pltpu.VMEM((chips - 1, toks, cols), bf16),
            dma((4,)),
            dma((rows,)),
            dma((2,)),
            dma((4,)),
            pltpu.SemaphoreType.REGULAR((2,)),
            dma((2,)),
            dma((2,)),
            dma((2, 2)),
            dma,
            dma,
            dma((chips,)),
            dma((chips,)),
            dma((chips - 1,)),
            dma((chips - 1,)),
        ],
        compiler_params=pltpu.CompilerParams(
            collective_id=0, has_side_effects=True, vmem_limit_bytes=VMEM_BYTES
        ),
    )(
        queries,
        keys[:, 0],
        values[:, 0],
        step_keys[:, :, 0],
        step_values[:, :, 0],
        lengths[None, :],
        weight,
        down.T,
        up,
    )


def solution(mesh):
    return jax.shard_map(
        functools.partial(on_device, (mesh.shape["group"], mesh.shape["tensor"])),
        mesh=mesh,
        in_specs=(
            P(None, "group", "tensor"),
            P("group", "tensor", None, None),
            P("group", "tensor", None, None),
            P(None, "group", "tensor", None),
            P(None, "group", "tensor", None),
            P("group"),
            P("tensor", None),
            P("tensor", "group"),
            P("group", "tensor"),
        ),
        out_specs=P(None, "group", "tensor"),
        check_vma=False,
    )
```

```python
import functools
import math

import jax
import jax.numpy as jnp
from jax import lax
from jax.experimental import pallas as pl
from jax.experimental.pallas import tpu as pltpu
from jax.sharding import PartitionSpec as P

MESH = pl.DeviceIdType.MESH
HEAD_SIZE = 128
QH = 2
EXP2_SCALE = HEAD_SIZE**-0.5 / math.log(2.0)
NEG = -1e30
VMEM_BYTES = 63 * 1024 * 1024


def nt_dot(a, b):
    return lax.dot_general(a, b, (((1,), (1,)), ((), ())), preferred_element_type=jnp.float32)


def kernel(
    groups,
    tensors,
    q_hbm,
    k_hbm,
    v_hbm,
    sk_hbm,
    sv_hbm,
    len_hbm,
    w_hbm,
    down_hbm,
    up_hbm,
    out_ref,
    q_v,
    k_v,
    v_v,
    sk_v,
    sv_v,
    len_v,
    w_v,
    down_v,
    up_v,
    gdown,
    gup,
    down_f,
    up_f,
    lows,
    keep,
    send1,
    recv1,
    send2,
    recv2,
    small_sem,
    k_sem,
    v_sem,
    w_sem,
    met_sem,
    mine_sem,
    sent_sem,
    come_sem,
    low_sent,
    low_sem,
    s1_sem,
    r1_sem,
    s2_sem,
    r2_sem,
):
    steps, rows, _ = q_v.shape
    cache = k_v.shape[0]
    toks = steps * rows
    cols = out_ref.shape[2]
    chips = tensors // 2
    rank = down_f.shape[0]

    g = lax.axis_index("group")
    t = lax.axis_index("tensor")
    chip = t // 2
    core = t % 2
    planes = groups // 2
    z = lax.rem(g, planes)
    order = 2 * z + g // planes
    late = (2 * z) // planes

    smalls = [
        pltpu.make_async_copy(src, dst, small_sem.at[i])
        for i, (src, dst) in enumerate(
            [
                (q_hbm, q_v),
                (sk_hbm, sk_v),
                (sv_hbm, sv_v),
                (len_hbm, len_v),
            ]
        )
    ]
    k_copies = [
        pltpu.make_async_copy(k_hbm.at[r], k_v.at[:, pl.ds(r * HEAD_SIZE, HEAD_SIZE)], k_sem.at[r])
        for r in range(rows)
    ]
    v_copies = [
        pltpu.make_async_copy(v_hbm.at[part], v_v.at[part], v_sem.at[i])
        for i, part in enumerate((pl.ds(0, rows // 2), pl.ds(rows // 2, rows // 2)))
    ]
    pair = 2 * cols

    def chunk_at(k):
        return lax.rem(chip + k + 1, chips)

    depth = w_v.shape[0]
    w_copies = [
        pltpu.make_async_copy(w_hbm.at[part], w_v.at[part], w_sem.at[i])
        for i, part in enumerate(pl.ds(i * (depth // 4), depth // 4) for i in range(4))
    ]
    mine_copies = [
        pltpu.make_async_copy(down_hbm, down_v, mine_sem.at[0]),
        pltpu.make_async_copy(up_hbm, up_v, mine_sem.at[1]),
    ]
    for c in mine_copies:
        c.start()


    barrier = pltpu.get_barrier_semaphore()
    home = t - core
    partner = {"tensor": home + 1 - core}
    half = groups // 2
    first_mail = late
    hurry = 4 * z >= planes
    calm = jnp.where(hurry, 0, 1)
    quarter = groups // 4
    plane = 2 * (chips - 1)

    @pl.when(core != first_mail)
    def _():
        pl.semaphore_signal(barrier, inc=1, device_id=partner, device_id_type=MESH)

    def group_at(k):
        return lax.rem(k, 2) * planes + k // 2

    def greet():
        def greet_group(i, carry):
            away = (i + 1) // 2 * (1 - 2 * lax.rem(i, 2))
            k = lax.rem(order + half + away + groups, groups)
            there = k // half
            mail = late + there - 2 * late * there
            mail = jnp.where(k < quarter, 1 - calm, mail)
            pl.semaphore_signal(
                barrier,
                inc=1,
                device_id={"group": group_at(k), "tensor": home + mail},
                device_id_type=MESH,
            )
            return carry

        lax.fori_loop(0, groups - 1, greet_group, 0)
        for k in range(chips - 1):
            pl.semaphore_signal(
                barrier,
                inc=1,
                device_id={"tensor": chunk_at(k) * 2 + (1 - late) * (1 - calm)},
                device_id_type=MESH,
            )

    def meet(which, mail, count):
        @pl.when(core == mail)
        def _():
            pl.semaphore_wait(barrier, count)
            pl.semaphore_signal(met_sem.at[which], inc=1, device_id=partner, device_id_type=MESH)

        @pl.when(core != mail)
        def _():
            pl.semaphore_wait(met_sem.at[which], 1)

    def meet_first():
        others = jnp.where(hurry, half - 1 + late, quarter - 1)
        meet(0, first_mail, 2 * others + 1 + calm * plane)

    def meet_second():
        others = jnp.where(hurry, half - late, groups - quarter)
        meet(1, 1 - first_mail, 2 * others + (1 - calm) * plane)

    def send_to(first, last, which):
        src, dst = ((down_v, gdown), (up_v, gup))[which]

        def send(k, carry):
            pltpu.make_async_remote_copy(
                src_ref=src,
                dst_ref=dst.at[order],
                send_sem=sent_sem.at[which],
                recv_sem=come_sem.at[which, late],
                device_id={"group": group_at(k)},
                device_id_type=MESH,
            ).start()
            return carry

        lax.fori_loop(first, jnp.clip(order, first, last), send, 0)
        lax.fori_loop(jnp.clip(order + 1, first, last), last, send, 0)

    def wait_mine():
        for c in mine_copies:
            c.wait()


    last = (late == 1) & (4 * z < 3 * planes)
    pl.when(jnp.logical_not(last))(greet)
    for c in smalls + k_copies + v_copies + w_copies:
        c.start(priority=1)
    wait_mine()

    @pl.when(hurry)
    def _():
        meet_first()
        send_to(0, half, 0)

    pl.when(last)(greet)

    for c in smalls:
        c.wait()
    q32 = jnp.concatenate([q_v[s].astype(jnp.float32) for s in range(steps)], axis=0)
    q64 = jnp.concatenate([q32[:, h * HEAD_SIZE : (h + 1) * HEAD_SIZE] for h in range(QH)], axis=0)
    height = QH * toks
    row_of = lax.broadcasted_iota(jnp.int32, (height, 1), 0) % rows
    step_of = (lax.broadcasted_iota(jnp.int32, (height, 1), 0) // rows) % steps
    q_wide = jnp.concatenate(
        [jnp.where(row_of == r, q64, 0.0).astype(jnp.bfloat16) for r in range(rows)], axis=1
    )
    sk = jnp.concatenate([sk_v[s].astype(jnp.float32) for s in range(steps)], axis=0)
    sv = jnp.concatenate([sv_v[s].astype(jnp.float32) for s in range(steps)], axis=0)
    recent = nt_dot(q64.astype(jnp.bfloat16), sk.astype(jnp.bfloat16))
    col = lax.broadcasted_iota(jnp.int32, (height, toks), 1)
    recent = jnp.where((col % rows == row_of) & (col // rows <= step_of), recent, NEG)
    lane = lax.broadcasted_iota(jnp.int32, (rows, rows), 1)
    sub = lax.broadcasted_iota(jnp.int32, (rows, rows), 0)
    lens = jnp.sum(
        jnp.where(lane == sub, jnp.broadcast_to(len_v[...], (rows, rows)), 0).astype(jnp.float32),
        axis=1,
        keepdims=True,
    )
    lens = jnp.concatenate([lens] * (QH * steps), axis=0)
    for c in k_copies:
        c.wait()
    cached = nt_dot(q_wide, k_v[...])
    position = lax.broadcasted_iota(jnp.int32, (height, cache), 1).astype(jnp.float32)
    cached = jnp.where(position < lens, cached, NEG)
    top = jnp.maximum(
        jnp.max(cached, axis=1, keepdims=True), jnp.max(recent, axis=1, keepdims=True)
    )
    cached = jnp.exp2((cached - top) * EXP2_SCALE)
    recent = jnp.exp2((recent - top) * EXP2_SCALE)
    norm = 1.0 / (
        jnp.sum(cached, axis=1, keepdims=True) + jnp.sum(recent, axis=1, keepdims=True)
    )
    cached = cached * norm
    recent = (recent * norm).astype(jnp.bfloat16)
    for c in v_copies:
        c.wait()
    mixed = jnp.dot(recent, sv.astype(jnp.bfloat16), preferred_element_type=jnp.float32)
    weights = jnp.concatenate(
        [jnp.where(row_of == r, cached, 0.0).astype(jnp.bfloat16) for r in range(rows)], axis=1
    )
    mixed = mixed + jnp.dot(
        weights, v_v[...].reshape(rows * cache, HEAD_SIZE), preferred_element_type=jnp.float32)
    attended = jnp.concatenate([mixed[h * toks : (h + 1) * toks] for h in range(QH)], axis=1)
    attended = attended.astype(jnp.bfloat16)

    pl.when(hurry)(lambda: send_to(0, half, 1))

    @pl.when(late == 1)
    def _():
        meet_second()
        send_to(half, groups, 0)

    for c in w_copies:
        c.wait()
    for k in range(chips):
        part = jnp.dot(
            attended, w_v[:, k * pair : (k + 1) * pair], preferred_element_type=jnp.float32
        )
        first, second = part[:, :cols], part[:, cols:]
        keep[k, :, :] = jnp.where(core == 0, first, second)
        send1[k, :, :] = jnp.where(core == 0, second, first).astype(jnp.bfloat16)

    @pl.when(hurry & (late == 0))
    def _():
        meet_second()
        send_to(half, groups, 0)

    @pl.when(jnp.logical_not(hurry))
    def _():
        meet_first()
        send_to(0, quarter, 0)
        send_to(0, quarter, 1)


    to_partner = []
    for k in range(chips):
        copy = pltpu.make_async_remote_copy(
            src_ref=send1.at[chunk_at(k)],
            dst_ref=recv1.at[k],
            send_sem=s1_sem.at[k],
            recv_sem=r1_sem.at[k],
            device_id={"tensor": t + 1 - 2 * core},
            device_id_type=MESH,
        )
        copy.start()
        to_partner.append(copy)

    to_chips = []
    for k in range(chips):
        to_partner[k].wait_recv()
        both = keep[chunk_at(k)] + recv1[k].astype(jnp.float32)
        if k < chips - 1:
            send2[k, :, :] = both.astype(jnp.bfloat16)
            copy = pltpu.make_async_remote_copy(
                src_ref=send2.at[k],
                dst_ref=recv2.at[k],
                send_sem=s2_sem.at[k],
                recv_sem=r2_sem.at[k],
                device_id={"tensor": chunk_at(k) * 2 + core},
                device_id_type=MESH,
            )
            copy.start()
            to_chips.append(copy)
        else:
            total = both

    @pl.when(jnp.logical_not(hurry))
    def _():
        meet_second()
        send_to(quarter, groups, 0)

    gdown[order] = down_v[...]
    gup[order] = up_v[...]
    downs = gdown.at[pl.ds(0, groups - 1)]
    ups = gup.at[pl.ds(0, groups - 1)]

    def wait_half(which, buffer, h):
        for mine in (0, 1):
            blocks = buffer.at[pl.ds(0, half - mine)]

            @pl.when((late == h) == (mine == 1))
            def _():
                pltpu.make_async_copy(blocks, blocks, come_sem.at[which, h]).wait()


    per = gdown.shape[1]
    for h in range(2):
        wait_half(0, gdown, h)
        for i in range(h * half, (h + 1) * half):
            down_f[per * i : per * (i + 1), :] = gdown[i].astype(jnp.float32)
    low = nt_dot(attended, down_f[...].astype(jnp.bfloat16))
    top_rows = toks // 2
    low = jnp.concatenate([low[:top_rows], low[top_rows:]], axis=1)
    lows[tensors - 1, :, :] = low.astype(jnp.bfloat16)
    xs = chips // 2
    steps_away = sorted(
        ((a, b, c) for a in range(2) for b in range(xs) for c in range(2) if a + b + c),
        key=lambda s: (-2 * s[0] - min(s[1], xs - s[1]), s[2]),
    )
    far_first = [
        lax.rem(t // (2 * xs) + a, 2) * 2 * xs
        + lax.rem(lax.rem(chip, xs) + b, xs) * 2
        + lax.rem(core + c, 2)
        for a, b, c in steps_away
    ]
    low_copies = [
        pltpu.make_async_remote_copy(
            src_ref=lows.at[tensors - 1],
            dst_ref=lows.at[d],
            send_sem=low_sent,
            recv_sem=low_sem,
            device_id={"tensor": other},
            device_id_type=MESH,
        )
        for d, other in enumerate(far_first)
    ]
    for copy in low_copies:
        copy.start()

    pl.when(hurry)(lambda: send_to(half, groups, 1))
    pl.when(jnp.logical_not(hurry))(lambda: send_to(quarter, groups, 1))
    for h in range(2):
        wait_half(1, gup, h)
    for i in range(groups):
        up_f[per * i : per * (i + 1), :] = gup[i].astype(jnp.float32)
    up = up_f[...].astype(jnp.bfloat16)
    up = jnp.concatenate([up, up], axis=0)
    for k in range(chips - 1):
        to_chips[k].wait_recv()
        total = total + recv2[k].astype(jnp.float32)
    others = lows.at[pl.ds(0, tensors - 1)]
    pltpu.make_async_copy(others, others, low_sent).wait()
    pltpu.make_async_copy(downs, downs, sent_sem.at[0]).wait()
    pltpu.make_async_copy(ups, ups, sent_sem.at[1]).wait()
    for copy in to_partner + to_chips:
        copy.wait_send()

    pltpu.make_async_copy(others, others, low_sem).wait()
    low = lows[0].astype(jnp.float32)
    for d in range(1, tensors):
        low = low + lows[d].astype(jnp.float32)
    left = lax.broadcasted_iota(jnp.int32, low.shape, 1) < rank
    low = jnp.concatenate([jnp.where(left, low, 0.0), jnp.where(left, 0.0, low)], axis=0)
    high = low.astype(jnp.bfloat16)
    rest = (low - high.astype(jnp.float32)).astype(jnp.bfloat16)
    delta = jnp.dot(
        jnp.concatenate([high, rest], axis=0), up, preferred_element_type=jnp.float32
    )
    delta = delta[:toks] + delta[toks:]
    result = (total + 2.0 * delta).astype(out_ref.dtype)
    for s in range(steps):
        out_ref[s, :, :] = result[s * rows : (s + 1) * rows]

def on_device(mesh_shape, queries, keys, values, step_keys, step_values, lengths, weight, down, up):
    groups, tensors = mesh_shape
    steps, rows, width = queries.shape
    cache = keys.shape[2]
    depth, per = down.shape
    cols = up.shape[1]
    chips = tensors // 2
    toks = steps * rows
    rank = per * groups
    bf16, f32 = jnp.bfloat16, jnp.float32
    hbm = pl.BlockSpec(memory_space=pltpu.HBM)
    dma = pltpu.SemaphoreType.DMA
    return pl.pallas_call(
        functools.partial(kernel, groups, tensors),
        out_shape=pltpu.VMEM((steps, rows, cols), bf16),
        in_specs=[hbm] * 9,
        out_specs=pl.BlockSpec(memory_space=pltpu.VMEM),
        scratch_shapes=[
            pltpu.VMEM((steps, rows, width), bf16),
            pltpu.VMEM((cache, rows * HEAD_SIZE), bf16),
            pltpu.VMEM((rows, cache, HEAD_SIZE), bf16),
            pltpu.VMEM((steps, rows, HEAD_SIZE), bf16),
            pltpu.VMEM((steps, rows, HEAD_SIZE), bf16),
            pltpu.VMEM((1, rows), jnp.int32),
            pltpu.VMEM((depth, weight.shape[1]), bf16),
            pltpu.VMEM((per, depth), bf16),
            pltpu.VMEM((per, cols), bf16),
            pltpu.VMEM((groups, per, depth), bf16),
            pltpu.VMEM((groups, per, cols), bf16),
            pltpu.VMEM((rank, depth), f32),
            pltpu.VMEM((rank, cols), f32),
            pltpu.VMEM((tensors, toks // 2, 2 * rank), bf16),
            pltpu.VMEM((chips, toks, cols), f32),
            pltpu.VMEM((chips, toks, cols), bf16),
            pltpu.VMEM((chips, toks, cols), bf16),
            pltpu.VMEM((chips - 1, toks, cols), bf16),
            pltpu.VMEM((chips - 1, toks, cols), bf16),
            dma((4,)),
            dma((rows,)),
            dma((2,)),
            dma((4,)),
            pltpu.SemaphoreType.REGULAR((2,)),
            dma((2,)),
            dma((2,)),
            dma((2, 2)),
            dma,
            dma,
            dma((chips,)),
            dma((chips,)),
            dma((chips - 1,)),
            dma((chips - 1,)),
        ],
        compiler_params=pltpu.CompilerParams(
            collective_id=0, has_side_effects=True, vmem_limit_bytes=VMEM_BYTES
        ),
    )(
        queries,
        keys[:, 0],
        values[:, 0],
        step_keys[:, :, 0],
        step_values[:, :, 0],
        lengths[None, :],
        weight,
        down.T,
        up,
    )


def solution(mesh):
    return jax.shard_map(
        functools.partial(on_device, (mesh.shape["group"], mesh.shape["tensor"])),
        mesh=mesh,
        in_specs=(
            P(None, "group", "tensor"),
            P("group", "tensor", None, None),
            P("group", "tensor", None, None),
            P(None, "group", "tensor", None),
            P(None, "group", "tensor", None),
            P("group"),
            P("tensor", None),
            P("tensor", "group"),
            P("group", "tensor"),
        ),
        out_specs=P(None, "group", "tensor"),
        check_vma=False,
    )
```
